256 devices in a mesh: dp: 64 (over x, z, core), mp: 4 (over y).
Axes of the slice: x: 4, y: 4, z: 8, core: 2. Of those that a mesh axis runs over, the one named last changes fastest.
Arguments:
- waveform: bfloat16 [64, 4, 4, 41216], P('dp', 'mp'), may hold values from -6 to 6
- lengths: int32 [64, 4, 4], P('dp', 'mp'), may hold values from 1 to 63, as said below
- conv_first: bfloat16 [64, 1, 3, 3], replicated, may hold values from -2 to 2
- conv_second: bfloat16 [64, 64, 3, 3], replicated, may hold values from -0.25 to 0.25
- input_weight: bfloat16 [1280, 1536], replicated, may hold values from -0.15625 to 0.15625
- norm_gain: float32 [1536], replicated, may hold values from 0.1 to 1.9
- attention_in: bfloat16 [1536, 3, 1536], P(None, None, 'mp'), may hold values from -5.1031036 to 5.1031036
- attention_out: bfloat16 [1536, 1536], P('mp'), may hold values from -0.15625 to 0.15625
- send_slots: int32 [64, 64, 4, 4], P('dp', None, 'mp'), may hold values from -1 to 254, as said below
- receive_slots: int32 [64, 4, 128], P('dp', 'mp'), may hold values from 0 to 255, as said below
- segment_ids: int32 [64, 4, 128], P('dp'), may hold values from 0 to 1023, as said below
Outputs:
- encoded: bfloat16 [64, 4, 128, 1536], P('dp', 'mp')
The draws below stay inside these ranges and needn't reach their ends.
Inputs may be any that keep to these rules, and one draw needn't show every extreme that they name: `lengths`: in every draw one utterance of each lane m has 63 frames and one has 1. send_slots[i, j, m, c] is the row u * 64 + s of loader (i, m) carried in slot c to packed shard (j, m), or -1 for an empty slot; every frame s below its utterance's length is sent exactly once, and each loader sends at most 4 rows to one packed shard, exactly 4 in some cases of every draw. Each packed shard (j, m) receives exactly 128 rows, only from loaders (i, m); receive_slots[j, m, p] = i * 4 + c names a filled slot, each filled slot once, in order of loader i and then of the loader's rows. `segment_ids`: the id of utterance u of loader (i, m) is (m * 64 + i) * 4 + u; rows with equal ids of a group are consecutive and lie in one device's rows.
All inputs are finite; a program needn't handle non-finite values.
Results may differ from the reference program's by a relative error of at most 0.019.
Values may be sent and summed in bfloat16 or wider, within the bound.
A program may use at most 128 MiB of HBM per device.

```python
import math
import jax
import jax.numpy as jnp
from jax import lax

D = 1536
HEADS = 24
N_MEL = 80
N_FFT = 400
HOP = 160
CH = 64
UTT_DEV = 4
TOK_DEV = 128
HEAD_DIM = 64
MEL_SUB = 20
SLOT_ROWS = 64
WAVE_LEN = 41216
N_DP = 64
N_MP = 4


def packing_plan(key):
    capacity = 2 * TOK_DEV // N_DP
    half_count = N_DP // 2
    first_draw = jax.random.randint(jax.random.fold_in(key, 11), (N_MP, half_count, UTT_DEV), 0, SLOT_ROWS - 1)
    second_draw = jax.random.randint(jax.random.fold_in(key, 12), (N_MP, half_count, UTT_DEV), 0, SLOT_ROWS - 1)
    long_side = SLOT_ROWS - 1 - first_draw * second_draw // (SLOT_ROWS - 1)
    long_side = long_side.at[:, 0, UTT_DEV - 1].set(SLOT_ROWS - 1)
    short_side = SLOT_ROWS - long_side
    paired = jnp.concatenate([long_side, short_side], axis=1)

    def shuffle(lane_key):
        return jax.random.permutation(lane_key, N_DP)
    lane_keys = jax.random.split(jax.random.fold_in(key, 13), N_MP)
    orders = jax.vmap(shuffle)(lane_keys)
    lane_rows = jnp.arange(N_MP, dtype=jnp.int32)[:, None]
    by_loader = jnp.zeros((N_MP, N_DP, UTT_DEV), jnp.int32).at[lane_rows, orders].set(paired)
    lengths = jnp.transpose(by_loader, (1, 0, 2))
    loader_loads = jnp.sum(lengths, axis=2)
    starts = jnp.cumsum(loader_loads, axis=0) - loader_loads
    utter_starts = jnp.cumsum(lengths, axis=2) - lengths
    frame_index = jnp.arange(SLOT_ROWS, dtype=jnp.int32)[None, None, None, :]
    inside = frame_index < lengths[..., None]
    global_row = starts[:, :, None, None] + utter_starts[..., None] + frame_index
    span_index = global_row // capacity
    slot_index = global_row % capacity
    target = jnp.where(inside, span_index % N_DP, N_DP)
    position = span_index // N_DP * capacity + slot_index
    source = jnp.arange(N_DP, dtype=jnp.int32)[:, None, None, None]
    lane_index = jnp.arange(N_MP, dtype=jnp.int32)[None, :, None, None]
    utterance = jnp.arange(UTT_DEV, dtype=jnp.int32)[None, None, :, None]
    local_row = utterance * SLOT_ROWS + frame_index
    shape_full = target.shape
    send_table = jnp.full((N_DP, N_DP, N_MP, capacity), -1, jnp.int32).at[jnp.broadcast_to(source, shape_full), target, jnp.broadcast_to(lane_index, shape_full), slot_index].set(jnp.broadcast_to(local_row, shape_full), mode='drop')
    receive = jnp.zeros((N_DP, N_MP, TOK_DEV), jnp.int32).at[target, jnp.broadcast_to(lane_index, shape_full), position].set(jnp.broadcast_to(source * capacity + slot_index, shape_full), mode='drop')
    segments = jnp.zeros((N_DP, N_MP, TOK_DEV), jnp.int32).at[target, jnp.broadcast_to(lane_index, shape_full), position].set(jnp.broadcast_to((lane_index * N_DP + source) * UTT_DEV + utterance, shape_full), mode='drop')
    return (lengths, send_table, receive, segments)


def draw_lengths(key, part):
    return packing_plan(key)[0]


def draw_send_slots(key, part):
    return packing_plan(key)[1]


def draw_receive_slots(key, part):
    return packing_plan(key)[2]


def draw_segment_ids(key, part):
    return packing_plan(key)[3]


def draw_attention_in(key, part):
    key = jax.random.fold_in(key, 7)
    fan_scale = D ** (-0.5)
    query_part = jax.random.truncated_normal(jax.random.fold_in(key, 1), -4.0, 4.0, (D, D), jnp.float32) * fan_scale
    key_part = jax.random.truncated_normal(jax.random.fold_in(key, 2), -4.0, 4.0, (D, D), jnp.float32) * fan_scale
    value_part = jax.random.truncated_normal(jax.random.fold_in(key, 3), -4.0, 4.0, (D, D), jnp.float32) * fan_scale
    return jnp.stack([query_part, key_part, value_part], axis=1).astype(jnp.bfloat16)


def shard_levels(rng, extent, cuts, smallest, high):
    level, own = 1.0, jax.random.fold_in(rng, 6)
    for axis_at, blocks in cuts:
        heights = jnp.exp(jax.random.uniform(jax.random.fold_in(own, axis_at), (blocks,), jnp.float32, smallest / len(cuts), high / len(cuts)))
        level = level * jnp.repeat(heights, extent[axis_at] // blocks).reshape([-1 if axis == axis_at else 1 for axis in range(len(extent))])
    return level


def gaussian(stream_key, dims, scale, most, cuts=(), kind=jnp.bfloat16):
    loudness = shard_levels(stream_key, dims, cuts, -0.22, 0.18) if cuts else 1.0
    result = jax.random.normal(stream_key, dims, jnp.float32) * scale * loudness
    return jnp.minimum(jnp.maximum(result, -most), most).astype(kind)


def setup_inputs(seed: int = 0) -> dict:
    keys = jax.random.split(jax.random.key(seed), 12)
    waveform = gaussian(keys[0], (N_DP, N_MP, UTT_DEV, WAVE_LEN), 1.0, 6.0, ((0, 64), (1, 4)))
    lengths = draw_lengths(jax.random.fold_in(keys[11], 71), 0)
    conv_first = gaussian(keys[2], (CH, 1, 3, 3), 9 ** -0.5, 2.0)
    conv_second = gaussian(keys[3], (CH, CH, 3, 3), (9 * CH) ** -0.5, 0.25)
    input_weight = gaussian(keys[4], (CH * MEL_SUB, D), (CH * MEL_SUB) ** -0.5, 0.15625)
    norm_gain = jnp.clip(1.0 + 0.18 * jax.random.normal(keys[5], (D,), jnp.float32), 0.1, 1.9)
    attention_in = draw_attention_in(jax.random.fold_in(keys[11], 71), 0)
    attention_out = gaussian(keys[7], (D, D), D ** -0.5, 0.15625, ((0, 4),))
    send_slots = draw_send_slots(jax.random.fold_in(keys[11], 71), 0)
    receive_slots = draw_receive_slots(jax.random.fold_in(keys[11], 71), 0)
    segment_ids = draw_segment_ids(jax.random.fold_in(keys[11], 71), 0)
    return dict(waveform=waveform, lengths=lengths, conv_first=conv_first, conv_second=conv_second, input_weight=input_weight, norm_gain=norm_gain, attention_in=attention_in, attention_out=attention_out, send_slots=send_slots, receive_slots=receive_slots, segment_ids=segment_ids)


sample_rate = 16000.0
log_offset = 0.01

def hann_window(length):
    position = jnp.arange(length, dtype=jnp.float32)
    return 0.5 - 0.5 * jnp.cos(2.0 * math.pi * position / length)

def mel_weights(bin_count, window_size, channels):
    frequency = jnp.arange(bin_count, dtype=jnp.float32) * (sample_rate / window_size)
    mel_top = 2595.0 * math.log10(1.0 + 0.5 * sample_rate / 700.0)
    points = jnp.arange(channels + 2, dtype=jnp.float32) * (mel_top / (channels + 1))
    hertz_points = 700.0 * (jnp.power(10.0, points / 2595.0) - 1.0)
    lower_edge = hertz_points[:-2]
    centre = hertz_points[1:-1]
    upper_edge = hertz_points[2:]
    rising = (frequency[:, None] - lower_edge[None, :]) / (centre - lower_edge)[None, :]
    falling = (upper_edge[None, :] - frequency[:, None]) / (upper_edge - centre)[None, :]
    return jnp.maximum(0.0, jnp.minimum(rising, falling))

def frame_signal(signal, hop_size, window_size, frame_count):
    pieces = -(-window_size // hop_size)
    needed = hop_size * (frame_count + pieces)
    extra_zeros = max(needed - signal.shape[-1], 0)
    padded = jnp.pad(signal, ((0, 0), (0, extra_zeros)))[:, :needed]
    blocks = padded.reshape(signal.shape[0], frame_count + pieces, hop_size)
    joined = jnp.concatenate([blocks[:, offset:offset + frame_count, :] for offset in range(pieces)], axis=-1)
    return joined[:, :, :window_size]

def subsample(log_image, conv_first, conv_second):
    numbers = ('NCHW', 'OIHW', 'NCHW')
    hidden = lax.conv_general_dilated(log_image[:, None], conv_first, (2, 2), ((1, 1), (1, 1)), dimension_numbers=numbers, preferred_element_type=jnp.float32)
    hidden = jnp.maximum(hidden, 0.0).astype(jnp.bfloat16)
    output = lax.conv_general_dilated(hidden, conv_second, (2, 2), ((1, 1), (1, 1)), dimension_numbers=numbers, preferred_element_type=jnp.float32)
    output = jnp.maximum(output, 0.0).astype(jnp.bfloat16)
    utterances, channels, mel_bands, steps = output.shape
    return output.transpose(0, 3, 1, 2).reshape(utterances * steps, channels * mel_bands)

def layer_norm(inputs, norm_gain):
    values = inputs.astype(jnp.float32)
    centre = values - lax.optimization_barrier(jnp.mean(values, axis=-1, keepdims=True))
    spread = lax.optimization_barrier(jnp.mean(centre * centre, axis=-1, keepdims=True))
    return (centre * lax.rsqrt(spread + 1e-05) * norm_gain).astype(jnp.bfloat16)

def attend(queries, key_rows, value_rows, row_ids, head_size):
    scores = jnp.einsum('qhd,khd->hqk', queries.astype(jnp.float32), key_rows.astype(jnp.float32)) / math.sqrt(head_size)
    same_segment = row_ids[:, None] == row_ids[None, :]
    scores = jnp.where(same_segment[None], scores, -jnp.inf)
    largest = lax.optimization_barrier(jnp.max(scores, axis=-1, keepdims=True))
    exponent = jnp.exp(scores - largest)
    attention_weights = (exponent / lax.optimization_barrier(jnp.sum(exponent, axis=-1, keepdims=True))).astype(jnp.bfloat16)
    context = jnp.einsum('hqk,khd->qhd', attention_weights.astype(jnp.float32), value_rows.astype(jnp.float32))
    return context.astype(jnp.bfloat16).reshape(queries.shape[0], -1)

def frontend_one(loader_item, conv_first, conv_second, input_weight):
    signal, own_lengths = loader_item
    frame_count = 4 * SLOT_ROWS
    frames = frame_signal(signal.astype(jnp.float32), HOP, N_FFT, frame_count) * hann_window(N_FFT)
    spectrum = jnp.fft.rfft(frames, axis=-1)
    power_bins = (jnp.real(spectrum) ** 2 + jnp.imag(spectrum) ** 2) / N_FFT
    weights = mel_weights(N_FFT // 2 + 1, N_FFT, N_MEL)
    energy = jnp.einsum('ufk,km->umf', power_bins, weights, precision=lax.Precision.HIGHEST)
    audible = jnp.arange(frame_count, dtype=jnp.int32)[None, None, :] < 4 * own_lengths[:, None, None]
    log_image = jnp.where(audible, jnp.log(energy + log_offset), 0.0).astype(jnp.bfloat16)
    features = subsample(log_image, conv_first, conv_second)
    return jnp.dot(features, input_weight, preferred_element_type=jnp.float32).astype(jnp.bfloat16)

def reference(waveform, lengths, conv_first, conv_second, input_weight, norm_gain, attention_in, attention_out, send_slots, receive_slots, segment_ids):
    loaders = waveform.reshape(N_DP * N_MP, UTT_DEV, WAVE_LEN)
    loader_lengths = lengths.reshape(N_DP * N_MP, UTT_DEV)

    def run_loader(loader_item):
        return frontend_one(loader_item, conv_first, conv_second, input_weight)
    embedded = lax.map(run_loader, (loaders, loader_lengths))
    embedded = embedded.reshape(N_DP, N_MP, UTT_DEV * SLOT_ROWS, D)
    capacity = send_slots.shape[3]
    source = (receive_slots // capacity).astype(jnp.int32)
    slot_index = (receive_slots % capacity).astype(jnp.int32)
    target_index = jnp.arange(N_DP, dtype=jnp.int32)[:, None, None]
    lane_index = jnp.arange(N_MP, dtype=jnp.int32)[None, :, None]
    loader_row = send_slots[source, target_index, lane_index, slot_index]
    packed = embedded[source, lane_index, loader_row]
    blocks = packed.reshape(N_DP * N_MP, TOK_DEV, D)
    block_ids = segment_ids.reshape(N_DP * N_MP, TOK_DEV)
    projector = attention_in.reshape(D, 3 * D)

    def encode_block(block_item):
        input_rows, row_ids = block_item
        normed = layer_norm(input_rows, norm_gain)
        projected = jnp.dot(normed, projector, preferred_element_type=jnp.float32).astype(jnp.bfloat16)
        heads_view = projected.reshape(TOK_DEV, 3, HEADS, HEAD_DIM)
        context = attend(heads_view[:, 0], heads_view[:, 1], heads_view[:, 2], row_ids, HEAD_DIM)
        attended = jnp.dot(context, attention_out, preferred_element_type=jnp.float32)
        return (input_rows.astype(jnp.float32) + attended).astype(jnp.bfloat16)
    encoded = lax.map(encode_block, (blocks, block_ids))
    return encoded.reshape(N_DP, N_MP, TOK_DEV, D)
```

```python
import functools
import math

import jax
import jax.numpy as jnp
import ml_dtypes
import numpy as np
from jax import lax
from jax.experimental import pallas as pl
from jax.experimental.pallas import tpu as pltpu
from jax.sharding import PartitionSpec as P

N_MEL = 80
N_FFT = 400
HOP = 160
HEAD_DIM = 64
SLOT_ROWS = 64
CH = 64
MEL_HALF = 40
MEL_SUB = 20
STEP = 4 * HOP
ROW = 4 * N_MEL
WINDOW = 2 * ROW
MESH = pl.DeviceIdType.MESH
VMEM = pltpu.VMEM
BF16 = jnp.bfloat16
F32 = jnp.float32


def split_table(table):
    high = table.astype(ml_dtypes.bfloat16)
    low = (table - high.astype(np.float64)).astype(ml_dtypes.bfloat16)
    return high, low


def dft_tables():
    position = np.arange(N_FFT)[:, None]
    harmonic = np.arange(256)[None, :]
    angles = 2.0 * math.pi * ((position * harmonic) % N_FFT) / N_FFT
    window = (0.5 - 0.5 * np.cos(2.0 * math.pi * position / N_FFT)) / math.sqrt(N_FFT)
    inside = harmonic <= N_FFT // 2
    base = np.concatenate(
        [np.where(inside, np.cos(angles), 0.0), np.where(inside, -np.sin(angles), 0.0)], axis=1
    )
    table = np.zeros((4, 512, 512))
    for r in range(4):
        table[r, 32 * r : 32 * r + N_FFT] = base * window
    return split_table(table)


def mel_tables():
    frequency = np.arange(N_FFT // 2 + 1) * (16000.0 / N_FFT)
    mel_top = 2595.0 * math.log10(1.0 + 8000.0 / 700.0)
    points = np.arange(N_MEL + 2) * (mel_top / (N_MEL + 1))
    hertz = 700.0 * (10.0 ** (points / 2595.0) - 1.0)
    lower, centre, upper = hertz[:-2], hertz[1:-1], hertz[2:]
    rising = (frequency[:, None] - lower) / (centre - lower)
    falling = (upper - frequency[:, None]) / (upper - centre)
    weights = np.maximum(0.0, np.minimum(rising, falling))
    table = np.zeros((4, 256, WINDOW))
    for r in range(4):
        for half in range(2):
            start = half * ROW + r * N_MEL
            table[r, : N_FFT // 2 + 1, start : start + N_MEL] = weights
    return split_table(table)


def dot(a, b):
    return jnp.dot(a, b, preferred_element_type=F32)


def frontend_kernel(x, dft_high, dft_low, mel_high, mel_low, lengths, picks, out):
    rows = x.shape[0]
    energy = jnp.zeros((rows, WINDOW), F32)
    for r in range(4):
        samples = x[:, 128 * r : 128 * r + 512]
        spectrum = dot(samples, dft_high[r]) + dot(samples, dft_low[r])
        power = spectrum[:, :256] * spectrum[:, :256] + spectrum[:, 256:] * spectrum[:, 256:]
        high = power.astype(BF16)
        low = (power - high.astype(F32)).astype(BF16)
        energy += dot(high, mel_high[r]) + dot(low, mel_high[r]) + dot(high, mel_low[r])
    row = lax.broadcasted_iota(jnp.int32, (rows, 1), 0)
    limit = jnp.full((rows, 1), lengths[0], jnp.int32)
    for u in range(1, rows // SLOT_ROWS):
        limit = jnp.where(row >= u * SLOT_ROWS, lengths[u], limit)
    audible = row % SLOT_ROWS < limit
    image = jnp.where(audible, jnp.log(energy + 0.01), 0.0).astype(BF16)
    pick = picks[...]
    before = jnp.where(pick % SLOT_ROWS == 0, -1, pick - 1)
    column = lax.broadcasted_iota(jnp.int32, (pick.shape[0], rows), 1)
    take_own = (column == pick).astype(F32).astype(BF16)
    take_before = (column == before).astype(F32).astype(BF16)
    own = dot(take_own, image)
    earlier = dot(take_before, image)
    lane = lax.broadcasted_iota(jnp.int32, own.shape, 1)
    out[...] = jnp.where(lane < ROW, earlier, own).astype(BF16)


def exchange_kernel(count, x, out, send_sems, recv_sems, local_sem):
    me, lane = lax.axis_index("dp"), lax.axis_index("mp")
    barrier = pltpu.get_barrier_semaphore()

    @pl.loop(1, count)
    def _(d):
        pl.semaphore_signal(
            barrier, inc=1, device_id=(lax.rem(me + d, count), lane), device_id_type=MESH
        )

    own = pltpu.make_async_copy(x.at[me], out.at[me], local_sem)
    own.start()
    pl.semaphore_wait(barrier, count - 1)

    def copy_to(d):
        peer = lax.rem(me + d, count)
        return pltpu.make_async_remote_copy(
            src_ref=x.at[peer],
            dst_ref=out.at[me],
            send_sem=send_sems.at[d],
            recv_sem=recv_sems.at[d],
            device_id=(peer, lane),
            device_id_type=MESH,
        )

    @pl.loop(1, count)
    def _(d):
        copy_to(d).start()

    own.wait()

    @pl.loop(1, count)
    def _(d):
        source = lax.rem(me + count - d, count)
        pltpu.make_async_remote_copy(
            src_ref=x.at[source],
            dst_ref=out.at[source],
            send_sem=send_sems.at[d],
            recv_sem=recv_sems.at[d],
            device_id=(source, lane),
            device_id_type=MESH,
        ).wait_recv()

    @pl.loop(1, count)
    def _(d):
        copy_to(d).wait_send()


def group_barrier(me, dp, count):
    barrier = pltpu.get_barrier_semaphore()
    for d in range(1, count):
        pl.semaphore_signal(
            barrier, inc=1, device_id=(dp, lax.rem(me + d, count)), device_id_type=MESH
        )
    return barrier


def gather_kernel(count, received, arrivals, out, send_sems, recv_sems):
    dp, me = lax.axis_index("dp"), lax.axis_index("mp")
    barrier = group_barrier(me, dp, count)
    arrival = arrivals[...]
    column = lax.broadcasted_iota(jnp.int32, (arrival.shape[0], received.shape[0]), 1)
    take = (column == arrival).astype(F32).astype(BF16)
    out[0] = dot(take, received[...]).astype(BF16)
    pl.semaphore_wait(barrier, count - 1)
    copies = []
    for d in range(1, count):
        copy = pltpu.make_async_remote_copy(
            src_ref=out.at[0],
            dst_ref=out.at[count - d],
            send_sem=send_sems.at[d],
            recv_sem=recv_sems.at[count - d],
            device_id=(dp, lax.rem(me + d, count)),
            device_id_type=MESH,
        )
        copy.start()
        copies.append(copy)
    for d in range(1, count):
        pltpu.make_async_remote_copy(
            src_ref=out.at[0],
            dst_ref=out.at[d],
            send_sem=send_sems.at[d],
            recv_sem=recv_sems.at[d],
            device_id=(dp, lax.rem(me + d, count)),
            device_id_type=MESH,
        ).wait_recv()
    for copy in copies:
        copy.wait_send()


def context_kernel(count, x, out, send_sems, recv_sems, local_sem):
    dp, me = lax.axis_index("dp"), lax.axis_index("mp")
    barrier = group_barrier(me, dp, count)
    own = pltpu.make_async_copy(x.at[0], out.at[me], local_sem)
    own.start()
    pl.semaphore_wait(barrier, count - 1)
    copies = []
    for d in range(1, count):
        copy = pltpu.make_async_remote_copy(
            src_ref=x.at[d],
            dst_ref=out.at[me],
            send_sem=send_sems.at[d],
            recv_sem=recv_sems.at[count - d],
            device_id=(dp, lax.rem(me + d, count)),
            device_id_type=MESH,
        )
        copy.start()
        copies.append(copy)
    own.wait()
    for d in range(1, count):
        source = lax.rem(me + d, count)
        pltpu.make_async_remote_copy(
            src_ref=x.at[d],
            dst_ref=out.at[source],
            send_sem=send_sems.at[d],
            recv_sem=recv_sems.at[d],
            device_id=(dp, source),
            device_id_type=MESH,
        ).wait_recv()
    for copy in copies:
        copy.wait_send()


def tables_kernel(first, second, first_table, second_table):
    mel = lax.broadcasted_iota(jnp.int32, (N_MEL, MEL_HALF * CH), 0)
    band = lax.broadcasted_iota(jnp.int32, (N_MEL, MEL_HALF * CH), 1) // CH
    offset = mel - 2 * band + 1
    for t in range(3):
        rows = jnp.zeros(offset.shape, F32)
        for d in range(3):
            rows = jnp.where(offset == d, first[3 * t + d : 3 * t + d + 1, :], rows)
        first_table[t * N_MEL : (t + 1) * N_MEL, :] = rows.astype(BF16)
    first_table[3 * N_MEL :, :] = jnp.zeros((256 - 3 * N_MEL, MEL_HALF * CH), BF16)
    spread_row = lax.broadcasted_iota(jnp.int32, (CH, 4 * CH), 0)
    spread_column = lax.broadcasted_iota(jnp.int32, (CH, 4 * CH), 1)
    spread = (spread_row == spread_column // 4).astype(F32).astype(BF16)
    sub_band = lax.broadcasted_iota(jnp.int32, (CH, 4 * CH), 1) % 4
    for t in range(3):
        wide = [
            dot(second[(3 * t + d) * CH : (3 * t + d + 1) * CH, :], spread) for d in range(3)
        ]
        for k in range(10):
            block = jnp.zeros((CH, 4 * CH), F32)
            for d in range(3):
                block = jnp.where(2 * sub_band + d + 1 == k, wide[d], block)
            second_table[t, k * CH : (k + 1) * CH, :] = block.astype(BF16)


def block_kernel(
    windows,
    first_table,
    second_table,
    input_weight,
    norm_gain,
    attention_in,
    ids_row,
    ids_column,
    contexts,
    own_rows,
    shifted,
    hidden,
    features,
    embedded,
    normed,
    projected,
):
    blocks, per_block = windows.shape[0], windows.shape[1]
    rows = blocks * per_block
    width = MEL_HALF * CH
    model = input_weight.shape[1]
    shifted[:, :, 3 * N_MEL :] = jnp.zeros((3, rows, 256 - 3 * N_MEL), BF16)
    hidden[:, :, :128] = jnp.zeros((3, rows, 128), BF16)
    image = windows[...].reshape(rows, WINDOW)
    for t in range(3):
        start = (1 + 2 * t) * N_MEL
        shifted[t, :, : 3 * N_MEL] = image[:, start : start + 3 * N_MEL]
    for t in range(3):
        for n in range(width // 256):
            value = dot(shifted[t], first_table[:, n * 256 : (n + 1) * 256])
            hidden[t, :, 128 + n * 256 : 128 + (n + 1) * 256] = jnp.maximum(value, 0.0).astype(BF16)
    for g in range(5):
        value = dot(hidden[0, :, 512 * g : 512 * g + 640], second_table[0])
        value += dot(hidden[1, :, 512 * g : 512 * g + 640], second_table[1])
        value += dot(hidden[2, :, 512 * g : 512 * g + 640], second_table[2])
        features[:, 256 * g : 256 * (g + 1)] = jnp.maximum(value, 0.0).astype(BF16)
    for n in range(model // 256):
        embedded[:, n * 256 : (n + 1) * 256] = dot(
            features[...], input_weight[:, n * 256 : (n + 1) * 256]
        ).astype(BF16)
    own_rows[...] = embedded[:per_block, :]
    for b in range(blocks):
        values = embedded[b * per_block : (b + 1) * per_block, :].astype(F32)
        centre = values - jnp.mean(values, axis=-1, keepdims=True)
        spread = jnp.mean(centre * centre, axis=-1, keepdims=True)
        normed[b * per_block : (b + 1) * per_block, :] = (
            centre * lax.rsqrt(spread + 1e-05) * norm_gain[...]
        ).astype(BF16)
    local = attention_in.shape[2]
    for part in range(3):
        projected[part] = dot(normed[...], attention_in[part]).astype(BF16)
    lane = lax.broadcasted_iota(jnp.int32, (per_block, 128), 1)
    lower = lane < HEAD_DIM
    zero = jnp.zeros((per_block, 128), BF16)
    for b in range(blocks):
        same = ids_column[b] == ids_row[b]
        span = slice(b * per_block, (b + 1) * per_block)
        for pair in range(local // 128):
            lanes = slice(pair * 128, (pair + 1) * 128)
            query = projected[0, span, lanes]
            key = projected[1, span, lanes]
            value = projected[2, span, lanes]
            key_pair = jnp.concatenate(
                [jnp.where(lower, key, zero), jnp.where(lower, zero, key)], axis=0
            )
            value_pair = jnp.concatenate(
                [jnp.where(lower, value, zero), jnp.where(lower, zero, value)], axis=0
            )
            scores = lax.dot_general(
                query, key_pair, (((1,), (1,)), ((), ())), preferred_element_type=F32
            ) * (1.0 / math.sqrt(HEAD_DIM))
            weights = []
            for half in range(2):
                part = jnp.where(same, scores[:, half * per_block : (half + 1) * per_block], -jnp.inf)
                largest = jnp.max(part, axis=-1, keepdims=True)
                exponent = jnp.exp(part - largest)
                total = jnp.sum(exponent, axis=-1, keepdims=True)
                weights.append((exponent / total).astype(BF16))
            contexts[b, :, lanes] = dot(jnp.concatenate(weights, axis=1), value_pair).astype(BF16)


def output_kernel(contexts, weight, residual, out):
    share = contexts.shape[2]
    total = residual[...].astype(F32)
    for m in range(contexts.shape[0]):
        total += dot(contexts[m], weight[m * share : (m + 1) * share, :])
    out[...] = total.astype(BF16)


def in_vmem(count):
    return [pl.BlockSpec(memory_space=VMEM)] * count


def shape_of(shape, dtype=BF16):
    return jax.ShapeDtypeStruct(shape, dtype)


def params(limit=48, **more):
    return pltpu.CompilerParams(vmem_limit_bytes=limit * 2**20, **more)


def on_device(
    dp_count,
    mp_count,
    waveform,
    lengths,
    conv_first,
    conv_second,
    input_weight,
    norm_gain,
    attention_in,
    attention_out,
    send_slots,
    receive_slots,
    segment_ids,
):
    signal = waveform[0, 0]
    utterances = signal.shape[0]
    capacity = send_slots.shape[3]
    slots = dp_count * capacity
    per_block = receive_slots.shape[2]
    model = input_weight.shape[1]
    local = attention_in.shape[2]
    whole_out = lax.all_gather(attention_out, "mp", axis=0, tiled=True)

    covered = SLOT_ROWS * STEP
    main = signal[:, :covered].reshape(utterances, SLOT_ROWS, STEP)
    following = jnp.concatenate(
        [main[:, 1:, :256], signal[:, None, covered : covered + 256]], axis=1
    )
    samples = jnp.concatenate([main, following], axis=2).reshape(utterances * SLOT_ROWS, 896)
    dft_high, dft_low = dft_tables()
    mel_high, mel_low = mel_tables()
    outgoing = pl.pallas_call(
        frontend_kernel,
        out_shape=shape_of((slots, WINDOW)),
        in_specs=in_vmem(5) + [pl.BlockSpec(memory_space=pltpu.SMEM)] + in_vmem(1),
        out_specs=pl.BlockSpec(memory_space=VMEM),
        compiler_params=params(),
        name="frontend",
    )(
        samples,
        jnp.asarray(dft_high),
        jnp.asarray(dft_low),
        jnp.asarray(mel_high),
        jnp.asarray(mel_low),
        lengths[0, 0],
        send_slots[0, :, 0, :].reshape(slots, 1),
    )

    received = pl.pallas_call(
        functools.partial(exchange_kernel, dp_count),
        out_shape=shape_of((dp_count, capacity, WINDOW)),
        in_specs=in_vmem(1),
        out_specs=pl.BlockSpec(memory_space=VMEM),
        scratch_shapes=[
            pltpu.SemaphoreType.DMA((dp_count,)),
            pltpu.SemaphoreType.DMA((dp_count,)),
            pltpu.SemaphoreType.DMA,
        ],
        compiler_params=params(collective_id=0, has_side_effects=True),
        name="exchange",
    )(outgoing.reshape(dp_count, capacity, WINDOW))

    windows = pl.pallas_call(
        functools.partial(gather_kernel, mp_count),
        out_shape=shape_of((mp_count, per_block, WINDOW)),
        in_specs=in_vmem(2),
        out_specs=pl.BlockSpec(memory_space=VMEM),
        scratch_shapes=[
            pltpu.SemaphoreType.DMA((mp_count,)),
            pltpu.SemaphoreType.DMA((mp_count,)),
        ],
        compiler_params=params(collective_id=1, has_side_effects=True),
        name="gather",
    )(received.reshape(slots, WINDOW), receive_slots[0, 0].reshape(per_block, 1))

    first = conv_first.reshape(CH, 3, 3).transpose(2, 1, 0).reshape(9, CH).astype(F32)
    second = conv_second.transpose(3, 2, 1, 0).reshape(9 * CH, CH)
    first_table, second_table = pl.pallas_call(
        tables_kernel,
        out_shape=(shape_of((256, MEL_HALF * CH)), shape_of((3, 10 * CH, 4 * CH))),
        in_specs=in_vmem(2),
        out_specs=tuple(in_vmem(2)),
        compiler_params=params(),
        name="tables",
    )(jnp.tile(first, (1, MEL_HALF)), second)
    ordered_weight = (
        input_weight.reshape(CH, 5, 4, model).transpose(1, 0, 2, 3).reshape(CH * MEL_SUB, model)
    )
    me = lax.axis_index("mp")
    own_ids = jnp.roll(segment_ids[0], -me, axis=0)
    rows = mp_count * per_block
    contexts, own_rows = pl.pallas_call(
        block_kernel,
        out_shape=(shape_of((mp_count, per_block, local)), shape_of((per_block, model))),
        in_specs=in_vmem(8),
        out_specs=tuple(in_vmem(2)),
        scratch_shapes=[
            VMEM((3, rows, 256), BF16),
            VMEM((3, rows, 128 + MEL_HALF * CH), BF16),
            VMEM((rows, CH * MEL_SUB), BF16),
            VMEM((rows, model), BF16),
            VMEM((rows, model), BF16),
            VMEM((3, rows, local), BF16),
        ],
        compiler_params=params(),
        name="block",
    )(
        windows,
        first_table,
        second_table,
        ordered_weight,
        norm_gain.reshape(1, model),
        attention_in.transpose(1, 0, 2),
        own_ids.reshape(mp_count, 1, per_block),
        own_ids.reshape(mp_count, per_block, 1),
    )

    whole_contexts = pl.pallas_call(
        functools.partial(context_kernel, mp_count),
        out_shape=shape_of((mp_count, per_block, local)),
        in_specs=in_vmem(1),
        out_specs=pl.BlockSpec(memory_space=VMEM),
        scratch_shapes=[
            pltpu.SemaphoreType.DMA((mp_count,)),
            pltpu.SemaphoreType.DMA((mp_count,)),
            pltpu.SemaphoreType.DMA,
        ],
        compiler_params=params(collective_id=2, has_side_effects=True),
        name="contexts",
    )(contexts)

    encoded = pl.pallas_call(
        output_kernel,
        out_shape=shape_of((per_block, model)),
        in_specs=in_vmem(3),
        out_specs=pl.BlockSpec(memory_space=VMEM),
        compiler_params=params(),
        name="output",
    )(whole_contexts, whole_out, own_rows)
    return encoded.reshape(1, 1, per_block, model)


def solution(mesh):
    return jax.shard_map(
        functools.partial(on_device, mesh.shape["dp"], mesh.shape["mp"]),
        mesh=mesh,
        in_specs=(
            P("dp", "mp", None, None),
            P("dp", "mp", None),
            P(),
            P(),
            P(),
            P(),
            P(None, None, "mp"),
            P("mp", None),
            P("dp", None, "mp", None),
            P("dp", "mp", None),
            P("dp", None, None),
        ),
        out_specs=P("dp", "mp", None, None),
        check_vma=False,
    )
```

```python
import functools
import math

import jax
import jax.numpy as jnp
import ml_dtypes
import numpy as np
from jax import lax
from jax.experimental import pallas as pl
from jax.experimental.pallas import tpu as pltpu
from jax.sharding import PartitionSpec as P

N_MEL = 80
N_FFT = 400
HOP = 160
HEAD_DIM = 64
SLOT_ROWS = 64
CH = 64
MEL_HALF = 40
MEL_SUB = 20
STEP = 4 * HOP
ROW = 4 * N_MEL
WINDOW = 2 * ROW
MESH = pl.DeviceIdType.MESH
VMEM = pltpu.VMEM
BF16 = jnp.bfloat16
F32 = jnp.float32


def dft_table():
    position = np.arange(N_FFT)[:, None]
    harmonic = np.arange(256)[None, :]
    angles = 2.0 * math.pi * ((position * harmonic) % N_FFT) / N_FFT
    window = (0.5 - 0.5 * np.cos(2.0 * math.pi * position / N_FFT)) / math.sqrt(N_FFT)
    inside = harmonic <= N_FFT // 2
    base = np.concatenate(
        [np.where(inside, np.cos(angles), 0.0), np.where(inside, -np.sin(angles), 0.0)], axis=1
    )
    table = np.zeros((4, 512, 512))
    for r in range(4):
        table[r, 32 * r : 32 * r + N_FFT] = base * window
    return table.astype(ml_dtypes.bfloat16)


def mel_table():
    frequency = np.arange(N_FFT // 2 + 1) * (16000.0 / N_FFT)
    mel_top = 2595.0 * math.log10(1.0 + 8000.0 / 700.0)
    points = np.arange(N_MEL + 2) * (mel_top / (N_MEL + 1))
    hertz = 700.0 * (10.0 ** (points / 2595.0) - 1.0)
    lower, centre, upper = hertz[:-2], hertz[1:-1], hertz[2:]
    rising = (frequency[:, None] - lower) / (centre - lower)
    falling = (upper - frequency[:, None]) / (upper - centre)
    weights = np.maximum(0.0, np.minimum(rising, falling))
    table = np.zeros((4, 256, WINDOW))
    for r in range(4):
        for half in range(2):
            start = half * ROW + r * N_MEL
            table[r, : N_FFT // 2 + 1, start : start + N_MEL] = weights
    return table.astype(ml_dtypes.bfloat16)


def dot(a, b):
    return jnp.dot(a, b, preferred_element_type=F32)


def one_hot(condition):
    return condition.astype(F32).astype(BF16)


def iota(shape, dimension):
    return lax.broadcasted_iota(jnp.int32, shape, dimension)


def contract(a, b, dim_a, dim_b):
    return lax.dot_general(a, b, (((dim_a,), (dim_b,)), ((), ())), preferred_element_type=F32)


def frontend_kernel(
    count,
    wave,
    lengths,
    picks,
    arrivals,
    conv_first,
    conv_second,
    dft_hbm,
    mel_hbm,
    weight_hbm,
    attention_hbm,
    windows,
    first_table,
    second_table,
    weight,
    attention,
    dft,
    mel,
    raw,
    samples,
    rows,
    outgoing,
    incoming,
    send_sems,
    recv_sems,
    local_sems,
):
    me, lane = lax.axis_index("dp"), lax.axis_index("mp")
    capacity = picks.shape[0]
    utterances = wave.shape[0]
    frames = utterances * SLOT_ROWS
    barrier = pltpu.get_barrier_semaphore()

    @pl.loop(1, count)
    def _(d):
        pl.semaphore_signal(
            barrier, inc=1, device_id=(lax.rem(me + d, count), lane), device_id_type=MESH
        )

    load_dft = pltpu.make_async_copy(dft_hbm, dft, local_sems.at[0])
    load_mel = pltpu.make_async_copy(mel_hbm, mel, local_sems.at[1])
    load_weight = pltpu.make_async_copy(weight_hbm, raw, local_sems.at[2])
    load_attention = pltpu.make_async_copy(attention_hbm, attention, local_sems.at[3])
    load_dft.start()
    load_mel.start()
    load_weight.start()
    load_attention.start()

    for s in range(SLOT_ROWS):
        samples[utterances * s : utterances * (s + 1), :] = wave[:, STEP * s : STEP * s + 896]
    load_dft.wait()
    load_mel.wait()
    energy = jnp.zeros((frames, WINDOW), F32)
    for r in range(4):
        spectrum = dot(samples[:, 128 * r : 128 * r + 512], dft[r])
        power = spectrum[:, :256] * spectrum[:, :256] + spectrum[:, 256:] * spectrum[:, 256:]
        energy += dot(power.astype(BF16), mel[r])
    row = iota((frames, 1), 0)
    limit = jnp.full((frames, 1), lengths[0], jnp.int32)
    for u in range(1, utterances):
        limit = jnp.where(row % utterances == u, lengths[u], limit)
    image = jnp.where(row // utterances < limit, jnp.log(energy + 0.01), 0.0).astype(BF16)

    slots = count * capacity
    target = (me + iota((slots, count), 0) // capacity) % count
    chosen = contract(one_hot(iota((slots, count), 1) == target), picks[...].astype(F32).astype(BF16), 1, 1)
    chosen = jnp.where(
        iota((slots, capacity), 1) == iota((slots, capacity), 0) % capacity, chosen, 0.0
    )
    pick = jnp.sum(chosen, axis=1, keepdims=True).astype(jnp.int32)
    place = jnp.where(pick < 0, -SLOT_ROWS, pick % SLOT_ROWS * utterances + pick // SLOT_ROWS)
    column = iota((slots, frames), 1)
    own = dot(one_hot(column == place), image)
    earlier = dot(one_hot(column == place - utterances), image)
    rows[...] = jnp.where(iota(own.shape, 1) < ROW, earlier, own)
    for d in range(count):
        slab = rows[capacity * d : capacity * (d + 1), :].astype(BF16)
        if d == 0:
            incoming[0] = slab
        else:
            outgoing[d] = slab

    pl.semaphore_wait(barrier, count - 1)

    def copy_to(d):
        return pltpu.make_async_remote_copy(
            src_ref=outgoing.at[d],
            dst_ref=incoming.at[d],
            send_sem=send_sems.at[d],
            recv_sem=recv_sems.at[d],
            device_id=(lax.rem(me + d, count), lane),
            device_id_type=MESH,
        )

    @pl.loop(1, count)
    def _(d):
        copy_to(d).start()

    twice = one_hot(iota((CH, 2 * CH), 0) == iota((CH, 2 * CH), 1) % CH)
    taps = [dot(conv_first[d], twice) for d in range(3)]
    first_table[3 * N_MEL :, :] = jnp.zeros((256 - 3 * N_MEL, MEL_HALF * CH), BF16)
    offset = iota((N_MEL, 2 * CH), 0) - 2 * (iota((N_MEL, 2 * CH), 1) // CH) + 1
    for n in range(MEL_HALF // 2):
        for t in range(3):
            block = jnp.zeros(offset.shape, F32)
            for d in range(3):
                block = jnp.where(offset - 4 * n == d, taps[d][t : t + 1, :], block)
            first_table[t * N_MEL : (t + 1) * N_MEL, 2 * CH * n : 2 * CH * (n + 1)] = block.astype(BF16)
    spread = one_hot(iota((CH, 4 * CH), 0) == iota((CH, 4 * CH), 1) // 4)
    sub_band = iota((CH, 4 * CH), 1) % 4
    for t in range(3):
        wide = [contract(conv_second[d, t], spread, 0, 0) for d in range(3)]
        for k in range(10):
            block = jnp.zeros((CH, 4 * CH), F32)
            for d in range(3):
                block = jnp.where(2 * sub_band + d + 1 == k, wide[d], block)
            second_table[t, k * CH : (k + 1) * CH, :] = block.astype(BF16)
    span = 16 * MEL_SUB
    out_row, in_row = iota((span, span), 0), iota((span, span), 1)
    source = (out_row % 64 // 4) * MEL_SUB + out_row // 64 * 4 + out_row % 4
    order = one_hot(in_row == source)
    load_weight.wait()
    for block in range(4):
        value = dot(order, raw[block * span : (block + 1) * span, :]).astype(BF16)
        for g in range(5):
            weight[256 * g + 64 * block : 256 * g + 64 * (block + 1), :] = value[64 * g : 64 * (g + 1), :]
    load_attention.wait()

    arrival = arrivals[...]
    position = (me + count - arrival // capacity) % count * capacity + arrival % capacity
    take = (iota((slots, arrival.shape[1]), 0) == position).astype(F32)
    take = jnp.transpose(take).astype(BF16)

    @pl.loop(1, count)
    def _(d):
        copy_to(d).wait_recv()

    for d in range(count):
        rows[capacity * d : capacity * (d + 1), :] = incoming[d].astype(F32)
    windows[...] = dot(take, rows[...].astype(BF16)).astype(BF16)

    @pl.loop(1, count)
    def _(d):
        copy_to(d).wait_send()


def block_kernel(
    count,
    own_windows,
    first_table,
    second_table,
    weight,
    norm_gain,
    attention,
    ids,
    contexts,
    own_rows,
    windows,
    shifted,
    hidden,
    features,
    embedded,
    normed,
    projected,
    sending,
    gather_send,
    gather_recv,
    context_send,
    context_recv,
):
    dp, me = lax.axis_index("dp"), lax.axis_index("mp")
    per_block = own_windows.shape[0]
    rows = count * per_block
    width = MEL_HALF * CH
    model = weight.shape[1]
    local = attention.shape[2]
    barrier = pltpu.get_barrier_semaphore()
    for d in range(1, count):
        pl.semaphore_signal(
            barrier, inc=1, device_id=(dp, lax.rem(me + d, count)), device_id_type=MESH
        )

    def peer(d):
        return (dp, lax.rem(me + d, count))

    def gather_copy(d):
        return pltpu.make_async_remote_copy(
            src_ref=own_windows,
            dst_ref=windows.at[count - d],
            send_sem=gather_send.at[d],
            recv_sem=gather_recv.at[count - d],
            device_id=peer(d),
            device_id_type=MESH,
        )

    def gather_arrival(d):
        return pltpu.make_async_remote_copy(
            src_ref=own_windows,
            dst_ref=windows.at[d],
            send_sem=gather_send.at[d],
            recv_sem=gather_recv.at[d],
            device_id=peer(d),
            device_id_type=MESH,
        )

    def context_copy(d):
        return pltpu.make_async_remote_copy(
            src_ref=sending.at[d],
            dst_ref=contexts.at[me],
            send_sem=context_send.at[d],
            recv_sem=context_recv.at[count - d],
            device_id=peer(d),
            device_id_type=MESH,
        )

    def context_arrival(d):
        return pltpu.make_async_remote_copy(
            src_ref=sending.at[d],
            dst_ref=contexts.at[lax.rem(me + d, count)],
            send_sem=context_send.at[d],
            recv_sem=context_recv.at[d],
            device_id=peer(d),
            device_id_type=MESH,
        )

    lower = iota((per_block, 128), 1) < HEAD_DIM
    zero = jnp.zeros((per_block, 128), BF16)

    def project(start, stop, image):
        span = slice(start, stop)
        for t in range(3):
            first = (1 + 2 * t) * N_MEL
            shifted[t, span, : 3 * N_MEL] = image[:, first : first + 3 * N_MEL]
        for t in range(3):
            for n in range(width // 256):
                value = dot(shifted[t, span, :], first_table[:, n * 256 : (n + 1) * 256])
                hidden[t, span, 128 + n * 256 : 128 + (n + 1) * 256] = jnp.maximum(value, 0.0).astype(BF16)
        for g in range(5):
            value = dot(hidden[0, span, 512 * g : 512 * g + 640], second_table[0])
            value += dot(hidden[1, span, 512 * g : 512 * g + 640], second_table[1])
            value += dot(hidden[2, span, 512 * g : 512 * g + 640], second_table[2])
            features[span, 256 * g : 256 * (g + 1)] = jnp.maximum(value, 0.0).astype(BF16)
        for n in range(model // 256):
            embedded[span, n * 256 : (n + 1) * 256] = dot(
                features[span, :], weight[:, n * 256 : (n + 1) * 256]
            ).astype(BF16)
        for b in range(start, stop, per_block):
            values = embedded[b : b + per_block, :].astype(F32)
            centre = values - jnp.mean(values, axis=-1, keepdims=True)
            spread = jnp.mean(centre * centre, axis=-1, keepdims=True)
            normed[b : b + per_block, :] = (
                centre * lax.rsqrt(spread + 1e-05) * norm_gain[...]
            ).astype(BF16)
        for part in range(3):
            projected[part, span, :] = dot(normed[span, :], attention[part]).astype(BF16)

    def attend(b, store):
        block_ids = ids[pl.ds(lax.rem(me + b, count), 1), :]
        across = jnp.broadcast_to(block_ids, (per_block, per_block))
        same = across == jnp.transpose(across)
        span = slice(b * per_block, (b + 1) * per_block)
        for pair in range(local // 128):
            lanes = slice(pair * 128, (pair + 1) * 128)
            query = projected[0, span, lanes]
            key = projected[1, span, lanes]
            value = projected[2, span, lanes]
            key_pair = jnp.concatenate(
                [jnp.where(lower, key, zero), jnp.where(lower, zero, key)], axis=0
            )
            value_pair = jnp.concatenate(
                [jnp.where(lower, value, zero), jnp.where(lower, zero, value)], axis=0
            )
            scores = contract(query, key_pair, 1, 1) * (1.0 / math.sqrt(HEAD_DIM))
            weights = []
            for half in range(2):
                part = jnp.where(same, scores[:, half * per_block : (half + 1) * per_block], -jnp.inf)
                largest = jnp.max(part, axis=-1, keepdims=True)
                exponent = jnp.exp(part - largest)
                total = jnp.sum(exponent, axis=-1, keepdims=True)
                weights.append((exponent / total).astype(BF16))
            store(lanes, dot(jnp.concatenate(weights, axis=1), value_pair).astype(BF16))

    def store_own(lanes, value):
        contexts[me, :, lanes] = value

    shifted[:, :, 3 * N_MEL :] = jnp.zeros((3, rows, 256 - 3 * N_MEL), BF16)
    hidden[:, :, :128] = jnp.zeros((3, rows, 128), BF16)
    pl.semaphore_wait(barrier, count - 1)
    for d in range(1, count):
        gather_copy(d).start()
    project(0, per_block, own_windows[...])
    attend(0, store_own)
    own_rows[...] = embedded[:per_block, :]
    for d in range(1, count):
        gather_arrival(d).wait_recv()
    project(per_block, rows, windows[1:].reshape(rows - per_block, WINDOW))
    for d in range(1, count):

        def store_sending(lanes, value, d=d):
            sending[d, :, lanes] = value

        attend(d, store_sending)
        context_copy(d).start()
    for d in range(1, count):
        context_arrival(d).wait_recv()
    for d in range(1, count):
        gather_copy(d).wait_send()
        context_copy(d).wait_send()


def output_kernel(contexts, near, far, residual, out):
    core = lax.rem(lax.axis_index("dp"), 2)
    share = contexts.shape[2]
    half = near.shape[1]
    for index, part in ((core, near), (1 - core, far)):
        lanes = pl.ds(pl.multiple_of(index * half, 128), half)
        total = residual[:, lanes].astype(F32)
        for m in range(contexts.shape[0]):
            total += dot(contexts[m], part[m * share : (m + 1) * share, :])
        out[:, lanes] = total.astype(BF16)


def in_vmem(count):
    return [pl.BlockSpec(memory_space=VMEM)] * count


def in_any(count):
    return [pl.BlockSpec(memory_space=pl.ANY)] * count


def shape_of(shape, dtype=BF16):
    return jax.ShapeDtypeStruct(shape, dtype)


def params(limit=48, **more):
    return pltpu.CompilerParams(vmem_limit_bytes=limit * 2**20, **more)


def on_device(
    dp_count,
    mp_count,
    waveform,
    lengths,
    conv_first,
    conv_second,
    input_weight,
    norm_gain,
    attention_in,
    attention_out,
    send_slots,
    receive_slots,
    segment_ids,
):
    capacity = send_slots.shape[3]
    per_block = receive_slots.shape[2]
    model = input_weight.shape[1]
    local = attention_in.shape[2]
    half = model // 2
    rows = mp_count * per_block
    dma = pltpu.SemaphoreType.DMA

    core = lax.rem(lax.axis_index("dp"), 2)
    own_half = lax.dynamic_slice_in_dim(attention_out, core * half, half, axis=1)
    near = lax.all_gather(own_half, "mp", axis=0, tiled=True)
    far = lax.ppermute(near, "dp", [(i, i ^ 1) for i in range(dp_count)])

    windows, first_table, second_table, weight, attention = pl.pallas_call(
        functools.partial(frontend_kernel, dp_count),
        out_shape=(
            shape_of((per_block, WINDOW)),
            shape_of((256, MEL_HALF * CH)),
            shape_of((3, 10 * CH, 4 * CH)),
            shape_of((CH * MEL_SUB, model)),
            shape_of((3, model, local)),
        ),
        in_specs=in_vmem(1) + [pl.BlockSpec(memory_space=pltpu.SMEM)] + in_vmem(4) + in_any(4),
        out_specs=tuple(in_vmem(5)),
        scratch_shapes=[
            VMEM((4, 512, 512), BF16),
            VMEM((4, 256, WINDOW), BF16),
            VMEM((CH * MEL_SUB, model), BF16),
            VMEM((4 * SLOT_ROWS, 896), BF16),
            VMEM((dp_count * capacity, WINDOW), F32),
            VMEM((dp_count, capacity, WINDOW), BF16),
            VMEM((dp_count, capacity, WINDOW), BF16),
            dma((dp_count,)),
            dma((dp_count,)),
            dma((4,)),
        ],
        compiler_params=params(collective_id=0, has_side_effects=True),
        name="frontend",
    )(
        waveform[0, 0],
        lengths[0, 0],
        send_slots[0, :, 0, :].transpose(1, 0),
        receive_slots[0],
        conv_first.transpose(1, 2, 3, 0)[0],
        conv_second.transpose(2, 3, 0, 1),
        jnp.asarray(dft_table()),
        jnp.asarray(mel_table()),
        input_weight,
        attention_in.transpose(1, 0, 2),
    )

    contexts, own_rows = pl.pallas_call(
        functools.partial(block_kernel, mp_count),
        out_shape=(shape_of((mp_count, per_block, local)), shape_of((per_block, model))),
        in_specs=in_vmem(7),
        out_specs=tuple(in_vmem(2)),
        scratch_shapes=[
            VMEM((mp_count, per_block, WINDOW), BF16),
            VMEM((3, rows, 256), BF16),
            VMEM((3, rows, 128 + MEL_HALF * CH), BF16),
            VMEM((rows, CH * MEL_SUB), BF16),
            VMEM((rows, model), BF16),
            VMEM((rows, model), BF16),
            VMEM((3, rows, local), BF16),
            VMEM((mp_count, per_block, local), BF16),
            dma((mp_count,)),
            dma((mp_count,)),
            dma((mp_count,)),
            dma((mp_count,)),
        ],
        compiler_params=params(collective_id=1, has_side_effects=True),
        name="block",
    )(
        windows,
        first_table,
        second_table,
        weight,
        norm_gain.reshape(1, model),
        attention,
        segment_ids[0],
    )

    encoded = pl.pallas_call(
        output_kernel,
        out_shape=shape_of((per_block, model)),
        in_specs=in_vmem(4),
        out_specs=pl.BlockSpec(memory_space=VMEM),
        compiler_params=params(),
        name="output",
    )(contexts, near, far, own_rows)
    return encoded.reshape(1, 1, per_block, model)


def solution(mesh):
    return jax.shard_map(
        functools.partial(on_device, mesh.shape["dp"], mesh.shape["mp"]),
        mesh=mesh,
        in_specs=(
            P("dp", "mp", None, None),
            P("dp", "mp", None),
            P(),
            P(),
            P(),
            P(),
            P(None, None, "mp"),
            P("mp", None),
            P("dp", None, "mp", None),
            P("dp", "mp", None),
            P("dp", None, None),
        ),
        out_specs=P("dp", "mp", None, None),
        check_vma=False,
    )
```

```python
import functools
import math

import jax
import jax.numpy as jnp
import ml_dtypes
import numpy as np
from jax import lax
from jax.experimental import pallas as pl
from jax.experimental.pallas import tpu as pltpu
from jax.sharding import PartitionSpec as P

N_MEL = 80
N_FFT = 400
HOP = 160
HEAD_DIM = 64
SLOT_ROWS = 64
CH = 64
MEL_HALF = 40
MEL_SUB = 20
STEP = 4 * HOP
ROW = 4 * N_MEL
WINDOW = 2 * ROW
MESH = pl.DeviceIdType.MESH
VMEM = pltpu.VMEM
BF16 = jnp.bfloat16
F32 = jnp.float32


def dft_table():
    position = np.arange(N_FFT)[:, None]
    harmonic = np.arange(256)[None, :]
    angles = 2.0 * math.pi * ((position * harmonic) % N_FFT) / N_FFT
    window = (0.5 - 0.5 * np.cos(2.0 * math.pi * position / N_FFT)) / math.sqrt(N_FFT)
    inside = harmonic <= N_FFT // 2
    base = np.concatenate(
        [np.where(inside, np.cos(angles), 0.0), np.where(inside, -np.sin(angles), 0.0)], axis=1
    )
    table = np.zeros((4, 512, 512))
    for r in range(4):
        table[r, 32 * r : 32 * r + N_FFT] = base * window
    return table.astype(ml_dtypes.bfloat16)


def mel_table():
    frequency = np.arange(N_FFT // 2 + 1) * (16000.0 / N_FFT)
    mel_top = 2595.0 * math.log10(1.0 + 8000.0 / 700.0)
    points = np.arange(N_MEL + 2) * (mel_top / (N_MEL + 1))
    hertz = 700.0 * (10.0 ** (points / 2595.0) - 1.0)
    lower, centre, upper = hertz[:-2], hertz[1:-1], hertz[2:]
    rising = (frequency[:, None] - lower) / (centre - lower)
    falling = (upper - frequency[:, None]) / (upper - centre)
    weights = np.maximum(0.0, np.minimum(rising, falling))
    table = np.zeros((4, 256, WINDOW))
    for r in range(4):
        for half in range(2):
            start = half * ROW + r * N_MEL
            table[r, : N_FFT // 2 + 1, start : start + N_MEL] = weights
    return table.astype(ml_dtypes.bfloat16)


def dot(a, b):
    return jnp.dot(a, b, preferred_element_type=F32)


def one_hot(condition):
    return condition.astype(F32).astype(BF16)


def iota(shape, dimension):
    return lax.broadcasted_iota(jnp.int32, shape, dimension)


def contract(a, b, dim_a, dim_b):
    return lax.dot_general(a, b, (((dim_a,), (dim_b,)), ((), ())), preferred_element_type=F32)


def solution_kernel(
    dp_count,
    mp_count,
    wave_hbm,
    lengths_hbm,
    picks_hbm,
    arrivals_hbm,
    first_hbm,
    second_hbm,
    dft_hbm,
    mel_hbm,
    weight_hbm,
    gain_hbm,
    attention_hbm,
    output_hbm,
    ids_hbm,
    encoded,
    wave,
    lengths,
    picks,
    arrivals,
    conv_first,
    conv_second,
    dft,
    mel,
    raw,
    norm_gain,
    attention,
    near,
    far,
    ids,
    first_table,
    second_table,
    weight,
    samples,
    slots_rows,
    outgoing,
    incoming,
    windows,
    shifted,
    hidden,
    features,
    embedded,
    normed,
    projected,
    sending,
    contexts,
    load_sems,
    exchange_send,
    exchange_recv,
    gather_send,
    gather_recv,
    near_send,
    near_recv,
    far_send,
    far_recv,
    context_send,
    context_recv,
):
    dp, me = lax.axis_index("dp"), lax.axis_index("mp")
    core = lax.rem(dp, 2)
    capacity = picks.shape[0]
    utterances = wave.shape[0]
    frames = utterances * SLOT_ROWS
    slots = dp_count * capacity
    per_block = windows.shape[1]
    rows = mp_count * per_block
    model = weight.shape[1]
    local = attention.shape[2]
    half = model // 2
    width = MEL_HALF * CH

    barrier = pltpu.get_barrier_semaphore()

    @pl.loop(1, dp_count)
    def _(d):
        pl.semaphore_signal(
            barrier, inc=1, device_id=(lax.rem(dp + d, dp_count), me), device_id_type=MESH
        )

    for d in range(1, mp_count):
        pl.semaphore_signal(
            barrier, inc=1, device_id=(dp, lax.rem(me + d, mp_count)), device_id_type=MESH
        )

    own_output = output_hbm.at[:, pl.ds(pl.multiple_of(core * half, 128), half)]
    loads = [
        pltpu.make_async_copy(source, target, load_sems.at[index])
        for index, (source, target) in enumerate(
            (
                (wave_hbm, wave),
                (dft_hbm, dft),
                (mel_hbm, mel),
                (lengths_hbm, lengths),
                (picks_hbm, picks),
                (first_hbm, conv_first),
                (second_hbm, conv_second),
                (arrivals_hbm, arrivals),
                (ids_hbm, ids),
                (gain_hbm, norm_gain),
                (weight_hbm, raw),
                (attention_hbm, attention),
                (own_output, near.at[0]),
            )
        )
    ]
    for load in loads:
        load.start()

    loads[0].wait()
    for s in range(SLOT_ROWS):
        samples[utterances * s : utterances * (s + 1), :] = wave[:, STEP * s : STEP * s + 896]
    loads[1].wait()
    loads[2].wait()
    energy = jnp.zeros((frames, WINDOW), F32)
    for r in range(4):
        spectrum = dot(samples[:, 128 * r : 128 * r + 512], dft[r])
        power = spectrum[:, :256] * spectrum[:, :256] + spectrum[:, 256:] * spectrum[:, 256:]
        energy += dot(power.astype(BF16), mel[r])
    loads[3].wait()
    row = iota((frames, 1), 0)
    limit = jnp.broadcast_to(lengths[0:1, 0:1], (frames, 1))
    for u in range(1, utterances):
        limit = jnp.where(row % utterances == u, lengths[0:1, u : u + 1], limit)
    image = jnp.where(row // utterances < limit, jnp.log(energy + 0.01), 0.0).astype(BF16)

    loads[4].wait()
    target = (dp + iota((slots, dp_count), 0) // capacity) % dp_count
    chosen = contract(
        one_hot(iota((slots, dp_count), 1) == target), picks[...].astype(F32).astype(BF16), 1, 1
    )
    chosen = jnp.where(
        iota((slots, capacity), 1) == iota((slots, capacity), 0) % capacity, chosen, 0.0
    )
    pick = jnp.sum(chosen, axis=1, keepdims=True).astype(jnp.int32)
    place = jnp.where(pick < 0, -SLOT_ROWS, pick % SLOT_ROWS * utterances + pick // SLOT_ROWS)
    column = iota((slots, frames), 1)
    own = dot(one_hot(column == place), image)
    earlier = dot(one_hot(column == place - utterances), image)
    slots_rows[...] = jnp.where(iota(own.shape, 1) < ROW, earlier, own)
    for d in range(dp_count):
        slab = slots_rows[capacity * d : capacity * (d + 1), :].astype(BF16)
        if d == 0:
            incoming[0] = slab
        else:
            outgoing[d] = slab

    pl.semaphore_wait(barrier, dp_count - 1 + mp_count - 1)

    def exchange(d):
        return pltpu.make_async_remote_copy(
            src_ref=outgoing.at[d],
            dst_ref=incoming.at[d],
            send_sem=exchange_send.at[d],
            recv_sem=exchange_recv.at[d],
            device_id=(lax.rem(dp + d, dp_count), me),
            device_id_type=MESH,
        )

    def to_lane(source, target, send_sem, recv_sem, d):
        return pltpu.make_async_remote_copy(
            src_ref=source,
            dst_ref=target,
            send_sem=send_sem,
            recv_sem=recv_sem,
            device_id=(dp, lax.rem(me + d, mp_count)),
            device_id_type=MESH,
        )

    def to_sibling(d):
        return pltpu.make_async_remote_copy(
            src_ref=near.at[d],
            dst_ref=far.at[d],
            send_sem=far_send.at[d],
            recv_sem=far_recv.at[d],
            device_id=(dp + 1 - 2 * core, me),
            device_id_type=MESH,
        )

    @pl.loop(1, dp_count)
    def _(d):
        exchange(d).start()

    last = mp_count - 1
    share = local // 2
    near_out = [
        to_lane(own_output, near.at[last], near_send.at[0], near_recv.at[0], 1),
        to_lane(own_output, near.at[1], near_send.at[1], near_recv.at[1], last),
    ]
    near_on = [
        to_lane(near.at[last, :share], near.at[2, :share], near_send.at[2], near_recv.at[2], 1),
        to_lane(near.at[1, share:], near.at[2, share:], near_send.at[3], near_recv.at[3], last),
    ]
    for copy in near_out:
        copy.start()

    loads[5].wait()
    loads[6].wait()
    twice = one_hot(iota((CH, 2 * CH), 0) == iota((CH, 2 * CH), 1) % CH)
    taps = [dot(conv_first[d], twice) for d in range(3)]
    first_table[3 * N_MEL :, :] = jnp.zeros((256 - 3 * N_MEL, width), BF16)
    offset = iota((N_MEL, 2 * CH), 0) - 2 * (iota((N_MEL, 2 * CH), 1) // CH) + 1
    for n in range(MEL_HALF // 2):
        for t in range(3):
            block = jnp.zeros(offset.shape, F32)
            for d in range(3):
                block = jnp.where(offset - 4 * n == d, taps[d][t : t + 1, :], block)
            first_table[t * N_MEL : (t + 1) * N_MEL, 2 * CH * n : 2 * CH * (n + 1)] = block.astype(BF16)
    spread = one_hot(iota((CH, 4 * CH), 0) == iota((CH, 4 * CH), 1) // 4)
    sub_band = iota((CH, 4 * CH), 1) % 4
    for t in range(3):
        wide = [contract(conv_second[d, t], spread, 0, 0) for d in range(3)]
        for k in range(10):
            block = jnp.zeros((CH, 4 * CH), F32)
            for d in range(3):
                block = jnp.where(2 * sub_band + d + 1 == k, wide[d], block)
            second_table[t, k * CH : (k + 1) * CH, :] = block.astype(BF16)
    span = 16 * MEL_SUB
    out_row, in_row = iota((span, span), 0), iota((span, span), 1)
    source = (out_row % 64 // 4) * MEL_SUB + out_row // 64 * 4 + out_row % 4
    order = one_hot(in_row == source)
    loads[10].wait()
    for block in range(4):
        value = dot(order, raw[block * span : (block + 1) * span, :]).astype(BF16)
        for g in range(5):
            weight[256 * g + 64 * block : 256 * g + 64 * (block + 1), :] = value[64 * g : 64 * (g + 1), :]
    shifted[:, :, 3 * N_MEL :] = jnp.zeros((3, rows, 256 - 3 * N_MEL), BF16)
    hidden[:, :, :128] = jnp.zeros((3, rows, 128), BF16)

    loads[7].wait()
    loads[8].wait()
    loads[9].wait()
    loads[11].wait()
    loads[12].wait()
    arrival = arrivals[...]
    position = (dp + dp_count - arrival // capacity) % dp_count * capacity + arrival % capacity
    take = (iota((slots, per_block), 0) == position).astype(F32)
    take = jnp.transpose(take).astype(BF16)

    @pl.loop(1, dp_count)
    def _(d):
        exchange(d).wait_recv()

    for d in range(dp_count):
        slots_rows[capacity * d : capacity * (d + 1), :] = incoming[d].astype(F32)
    windows[0] = dot(take, slots_rows[...].astype(BF16)).astype(BF16)

    middle = per_block // 2
    window_out = [
        to_lane(windows.at[0], windows.at[last], gather_send.at[0], gather_recv.at[0], 1),
        to_lane(windows.at[0], windows.at[1], gather_send.at[1], gather_recv.at[1], last),
    ]
    window_on = [
        to_lane(windows.at[last, :middle], windows.at[2, :middle], gather_send.at[2], gather_recv.at[2], 1),
        to_lane(windows.at[1, middle:], windows.at[2, middle:], gather_send.at[3], gather_recv.at[3], last),
    ]
    for copy in window_out:
        copy.start()

    def convolve(start, stop, image):
        span = slice(start, stop)
        for t in range(3):
            first = (1 + 2 * t) * N_MEL
            shifted[t, span, : 3 * N_MEL] = image[:, first : first + 3 * N_MEL]
        for t in range(3):
            for n in range(width // 256):
                value = dot(shifted[t, span, :], first_table[:, n * 256 : (n + 1) * 256])
                hidden[t, span, 128 + n * 256 : 128 + (n + 1) * 256] = jnp.maximum(value, 0.0).astype(BF16)
        for g in range(5):
            value = dot(hidden[0, span, 512 * g : 512 * g + 640], second_table[0])
            value += dot(hidden[1, span, 512 * g : 512 * g + 640], second_table[1])
            value += dot(hidden[2, span, 512 * g : 512 * g + 640], second_table[2])
            features[span, 256 * g : 256 * (g + 1)] = jnp.maximum(value, 0.0).astype(BF16)

    def project(start, stop):
        span = slice(start, stop)
        for n in range(model // 256):
            embedded[span, n * 256 : (n + 1) * 256] = dot(
                features[span, :], weight[:, n * 256 : (n + 1) * 256]
            ).astype(BF16)
        gain = norm_gain[...].reshape(1, model)
        for b in range(start, stop, per_block):
            values = embedded[b : b + per_block, :].astype(F32)
            centre = values - jnp.mean(values, axis=-1, keepdims=True)
            variance = jnp.mean(centre * centre, axis=-1, keepdims=True)
            normed[b : b + per_block, :] = (centre * lax.rsqrt(variance + 1e-05) * gain).astype(BF16)
        for part in range(3):
            projected[part, span, :] = dot(normed[span, :], attention[part]).astype(BF16)

    lower = iota((per_block, 128), 1) < HEAD_DIM
    zero = jnp.zeros((per_block, 128), BF16)

    def attend(b, target):
        block_ids = ids[pl.ds(lax.rem(me + b, mp_count), 1), :]
        across = jnp.broadcast_to(block_ids, (per_block, per_block))
        same = across == jnp.transpose(across)
        span = slice(b * per_block, (b + 1) * per_block)
        for pair in range(local // 128):
            lanes = slice(pair * 128, (pair + 1) * 128)
            query = projected[0, span, lanes]
            key = projected[1, span, lanes]
            value = projected[2, span, lanes]
            key_pair = jnp.concatenate(
                [jnp.where(lower, key, zero), jnp.where(lower, zero, key)], axis=0
            )
            value_pair = jnp.concatenate(
                [jnp.where(lower, value, zero), jnp.where(lower, zero, value)], axis=0
            )
            scores = contract(query, key_pair, 1, 1) * (1.0 / math.sqrt(HEAD_DIM))
            weights = []
            for side in range(2):
                part = jnp.where(same, scores[:, side * per_block : (side + 1) * per_block], -jnp.inf)
                largest = jnp.max(part, axis=-1, keepdims=True)
                exponent = jnp.exp(part - largest)
                total = jnp.sum(exponent, axis=-1, keepdims=True)
                weights.append((exponent / total).astype(BF16))
            target[b, :, lanes] = dot(jnp.concatenate(weights, axis=1), value_pair).astype(BF16)

    convolve(0, per_block, windows[0])
    for copy in window_out:
        copy.wait_recv()
    for copy in window_on:
        copy.start()
    project(0, per_block)
    attend(0, contexts)
    for copy in window_on:
        copy.wait_recv()
    for copy in near_out:
        copy.wait_recv()
    for copy in near_on:
        copy.start()
    for d in (0, 1, last):
        to_sibling(d).start()
    convolve(per_block, rows, windows[1:].reshape(rows - per_block, WINDOW))
    project(per_block, rows)
    context_out = {}
    for d in (2, 1, last):
        attend(d, sending)
        context_out[d] = to_lane(
            sending.at[d],
            contexts.at[mp_count - d],
            context_send.at[d],
            context_recv.at[mp_count - d],
            d,
        )
        context_out[d].start()
    for copy in near_on:
        copy.wait_recv()
    to_sibling(2).start()
    for d in range(mp_count):
        to_sibling(d).wait_recv()

    sides = [embedded[:per_block, pl.ds(pl.multiple_of(index * half, 128), half)].astype(F32) for index in (core, 1 - core)]
    for d in (0, 2, 1, last):
        if d:
            to_lane(sending.at[d], contexts.at[d], context_send.at[d], context_recv.at[d], d).wait_recv()
        for index, part in enumerate((near, far)):
            sides[index] += dot(contexts[d], part[d])
    for index, value in zip((core, 1 - core), sides):
        encoded[:, pl.ds(pl.multiple_of(index * half, 128), half)] = value.astype(BF16)

    @pl.loop(1, dp_count)
    def _(d):
        exchange(d).wait_send()

    for copy in window_out + window_on + near_out + near_on + list(context_out.values()):
        copy.wait_send()
    for d in range(mp_count):
        to_sibling(d).wait_send()


def on_device(
    dp_count,
    mp_count,
    waveform,
    lengths,
    conv_first,
    conv_second,
    input_weight,
    norm_gain,
    attention_in,
    attention_out,
    send_slots,
    receive_slots,
    segment_ids,
):
    capacity = send_slots.shape[3]
    utterances = waveform.shape[2]
    per_block = receive_slots.shape[2]
    model = input_weight.shape[1]
    local = attention_in.shape[2]
    half = model // 2
    rows = mp_count * per_block
    slots = dp_count * capacity
    dma = pltpu.SemaphoreType.DMA
    operands = (
        waveform[0, 0],
        lengths[0],
        send_slots[0, :, 0, :].transpose(1, 0),
        receive_slots[0],
        conv_first.transpose(1, 2, 3, 0)[0],
        conv_second.transpose(2, 3, 0, 1),
        jnp.asarray(dft_table()),
        jnp.asarray(mel_table()),
        input_weight,
        norm_gain,
        attention_in.transpose(1, 0, 2),
        attention_out,
        segment_ids[0],
    )
    encoded = pl.pallas_call(
        functools.partial(solution_kernel, dp_count, mp_count),
        out_shape=jax.ShapeDtypeStruct((per_block, model), BF16),
        in_specs=[pl.BlockSpec(memory_space=pltpu.HBM)] * len(operands),
        out_specs=pl.BlockSpec(memory_space=VMEM),
        scratch_shapes=[
            VMEM(waveform.shape[2:], BF16),
            VMEM((1, utterances), jnp.int32),
            VMEM((capacity, dp_count), jnp.int32),
            VMEM((1, per_block), jnp.int32),
            VMEM((3, 3, CH), BF16),
            VMEM((3, 3, CH, CH), BF16),
            VMEM((4, 512, 512), BF16),
            VMEM((4, 256, WINDOW), BF16),
            VMEM((CH * MEL_SUB, model), BF16),
            VMEM((model,), F32),
            VMEM((3, model, local), BF16),
            VMEM((mp_count, local, half), BF16),
            VMEM((mp_count, local, half), BF16),
            VMEM((mp_count, per_block), jnp.int32),
            VMEM((256, MEL_HALF * CH), BF16),
            VMEM((3, 10 * CH, 4 * CH), BF16),
            VMEM((CH * MEL_SUB, model), BF16),
            VMEM((utterances * SLOT_ROWS, 896), BF16),
            VMEM((slots, WINDOW), F32),
            VMEM((dp_count, capacity, WINDOW), BF16),
            VMEM((dp_count, capacity, WINDOW), BF16),
            VMEM((mp_count, per_block, WINDOW), BF16),
            VMEM((3, rows, 256), BF16),
            VMEM((3, rows, 128 + MEL_HALF * CH), BF16),
            VMEM((rows, CH * MEL_SUB), BF16),
            VMEM((rows, model), BF16),
            VMEM((rows, model), BF16),
            VMEM((3, rows, local), BF16),
            VMEM((mp_count, per_block, local), BF16),
            VMEM((mp_count, per_block, local), BF16),
            dma((13,)),
            dma((dp_count,)),
            dma((dp_count,)),
            dma((4,)),
            dma((4,)),
            dma((4,)),
            dma((4,)),
            dma((mp_count,)),
            dma((mp_count,)),
            dma((mp_count,)),
            dma((mp_count,)),
        ],
        compiler_params=pltpu.CompilerParams(
            vmem_limit_bytes=60 * 2**20, collective_id=0, has_side_effects=True
        ),
        name="encode",
    )(*operands)
    return encoded.reshape(1, 1, per_block, model)


def solution(mesh):
    return jax.shard_map(
        functools.partial(on_device, mesh.shape["dp"], mesh.shape["mp"]),
        mesh=mesh,
        in_specs=(
            P("dp", "mp", None, None),
            P("dp", "mp", None),
            P(),
            P(),
            P(),
            P(),
            P(None, None, "mp"),
            P("mp", None),
            P("dp", None, "mp", None),
            P("dp", "mp", None),
            P("dp", None, None),
        ),
        out_specs=P("dp", "mp", None, None),
        check_vma=False,
    )
```

```python
import functools
import math

import jax
import jax.numpy as jnp
import ml_dtypes
import numpy as np
from jax import lax
from jax.experimental import pallas as pl
from jax.experimental.pallas import tpu as pltpu
from jax.sharding import PartitionSpec as P

N_MEL = 80
N_FFT = 400
HOP = 160
HEAD_DIM = 64
SLOT_ROWS = 64
CH = 64
MEL_HALF = 40
MEL_SUB = 20
STEP = 4 * HOP
ROW = 4 * N_MEL
WINDOW = 2 * ROW
X_CHIPS = 4
MESH = pl.DeviceIdType.MESH
VMEM = pltpu.VMEM
BF16 = jnp.bfloat16
F32 = jnp.float32


def dft_table():
    position = np.arange(N_FFT)[:, None]
    harmonic = np.arange(256)[None, :]
    angles = 2.0 * math.pi * ((position * harmonic) % N_FFT) / N_FFT
    window = (0.5 - 0.5 * np.cos(2.0 * math.pi * position / N_FFT)) / math.sqrt(N_FFT)
    inside = harmonic <= N_FFT // 2
    base = np.concatenate(
        [np.where(inside, np.cos(angles), 0.0), np.where(inside, -np.sin(angles), 0.0)], axis=1
    )
    table = np.zeros((4, 512, 512))
    for r in range(4):
        table[r, 32 * r : 32 * r + N_FFT] = base * window
    return table.astype(ml_dtypes.bfloat16)


def mel_table():
    frequency = np.arange(N_FFT // 2 + 1) * (16000.0 / N_FFT)
    mel_top = 2595.0 * math.log10(1.0 + 8000.0 / 700.0)
    points = np.arange(N_MEL + 2) * (mel_top / (N_MEL + 1))
    hertz = 700.0 * (10.0 ** (points / 2595.0) - 1.0)
    lower, centre, upper = hertz[:-2], hertz[1:-1], hertz[2:]
    rising = (frequency[:, None] - lower) / (centre - lower)
    falling = (upper - frequency[:, None]) / (upper - centre)
    weights = np.maximum(0.0, np.minimum(rising, falling))
    table = np.zeros((4, 256, WINDOW))
    for r in range(4):
        for half in range(2):
            start = half * ROW + r * N_MEL
            table[r, : N_FFT // 2 + 1, start : start + N_MEL] = weights
    return table.astype(ml_dtypes.bfloat16)


def dot(a, b):
    return jnp.dot(a, b, preferred_element_type=F32)


def one_hot(condition):
    return condition.astype(F32).astype(BF16)


def iota(shape, dimension):
    return lax.broadcasted_iota(jnp.int32, shape, dimension)


def contract(a, b, dim_a, dim_b):
    return lax.dot_general(a, b, (((dim_a,), (dim_b,)), ((), ())), preferred_element_type=F32)


def solution_kernel(
    dp_count,
    mp_count,
    wave_hbm,
    lengths_hbm,
    picks_hbm,
    arrivals_hbm,
    first_hbm,
    second_hbm,
    dft_hbm,
    mel_hbm,
    weight_hbm,
    gain_hbm,
    attention_hbm,
    output_hbm,
    ids_hbm,
    encoded,
    wave,
    lengths,
    picks,
    arrivals,
    conv_first,
    conv_second,
    dft,
    mel,
    raw,
    norm_gain,
    attention,
    near,
    far,
    ids,
    first_table,
    second_table,
    weight,
    samples,
    slots_rows,
    outgoing,
    incoming,
    windows,
    shifted,
    hidden,
    features,
    embedded,
    normed,
    projected,
    sending,
    contexts,
    load_sems,
    exchange_send,
    exchange_recv,
    gather_send,
    gather_recv,
    near_send,
    near_recv,
    ring_send,
    ring_recv,
    far_send,
    far_recv,
    context_send,
    context_recv,
):
    dp, me = lax.axis_index("dp"), lax.axis_index("mp")
    core = lax.rem(dp, 2)
    capacity = picks.shape[0]
    utterances = wave.shape[0]
    frames = utterances * SLOT_ROWS
    slots = dp_count * capacity
    per_block = windows.shape[1]
    rows = mp_count * per_block
    model = weight.shape[1]
    local = attention.shape[1] // 3
    half = model // 2
    width = MEL_HALF * CH

    own_output = output_hbm.at[:, pl.ds(pl.multiple_of(core * half, 128), half)]
    plan = [
        (wave_hbm, wave),
        (dft_hbm, dft),
        (mel_hbm, mel),
        (lengths_hbm, lengths),
        (picks_hbm, picks),
        (first_hbm, conv_first),
        (second_hbm, conv_second),
        (arrivals_hbm, arrivals),
        (ids_hbm, ids),
        (gain_hbm, norm_gain),
        (weight_hbm, raw),
        (own_output, near.at[0]),
    ]
    for part in range(3):
        plan.append((attention_hbm.at[part], attention.at[:, part * local : (part + 1) * local]))
    loads = [
        pltpu.make_async_copy(source, target, load_sems.at[index])
        for index, (source, target) in enumerate(plan)
    ]
    for load in loads[:5]:
        load.start()

    barrier = pltpu.get_barrier_semaphore()

    @pl.loop(1, dp_count)
    def _(d):
        pl.semaphore_signal(
            barrier, inc=1, device_id=(lax.rem(dp + d, dp_count), me), device_id_type=MESH
        )

    for d in range(1, mp_count):
        pl.semaphore_signal(
            barrier, inc=1, device_id=(dp, lax.rem(me + d, mp_count)), device_id_type=MESH
        )

    for load in loads[5:]:
        load.start()

    loads[0].wait()
    for s in range(SLOT_ROWS):
        samples[utterances * s : utterances * (s + 1), :] = wave[:, STEP * s : STEP * s + 896]
    loads[1].wait()
    loads[2].wait()
    energy = jnp.zeros((frames, WINDOW), F32)
    for r in range(4):
        spectrum = dot(samples[:, 128 * r : 128 * r + 512], dft[r])
        power = spectrum[:, :256] * spectrum[:, :256] + spectrum[:, 256:] * spectrum[:, 256:]
        energy += dot(power.astype(BF16), mel[r])
    loads[3].wait()
    row = iota((frames, 1), 0)
    limit = jnp.broadcast_to(lengths[0:1, 0:1], (frames, 1))
    for u in range(1, utterances):
        limit = jnp.where(row % utterances == u, lengths[0:1, u : u + 1], limit)
    image = jnp.where(row // utterances < limit, jnp.log(energy + 0.01), 0.0).astype(BF16)

    loads[4].wait()
    target = (dp + iota((slots, dp_count), 0) // capacity) % dp_count
    chosen = contract(
        one_hot(iota((slots, dp_count), 1) == target), picks[...].astype(F32).astype(BF16), 1, 1
    )
    chosen = jnp.where(
        iota((slots, capacity), 1) == iota((slots, capacity), 0) % capacity, chosen, 0.0
    )
    pick = jnp.sum(chosen, axis=1, keepdims=True).astype(jnp.int32)
    place = jnp.where(pick < 0, -SLOT_ROWS, pick % SLOT_ROWS * utterances + pick // SLOT_ROWS)
    column = iota((slots, frames), 1)
    own = dot(one_hot(column == place), image)
    earlier = dot(one_hot(column == place - utterances), image)
    slots_rows[...] = jnp.where(iota(own.shape, 1) < ROW, earlier, own)
    for d in range(dp_count):
        slab = slots_rows[capacity * d : capacity * (d + 1), :].astype(BF16)
        if d == 0:
            incoming[0] = slab
        else:
            outgoing[d] = slab

    pl.semaphore_wait(barrier, dp_count - 1 + mp_count - 1)

    def exchange(d):
        return pltpu.make_async_remote_copy(
            src_ref=outgoing.at[d],
            dst_ref=incoming.at[d],
            send_sem=exchange_send.at[d],
            recv_sem=exchange_recv.at[d],
            device_id=(lax.rem(dp + d, dp_count), me),
            device_id_type=MESH,
        )

    def to_lane(source, target, send_sem, recv_sem, d):
        return pltpu.make_async_remote_copy(
            src_ref=source,
            dst_ref=target,
            send_sem=send_sem,
            recv_sem=recv_sem,
            device_id=(dp, lax.rem(me + d, mp_count)),
            device_id_type=MESH,
        )

    stride = dp_count // X_CHIPS
    ring = dp // stride
    quarter = local // 4
    parity = lax.rem(ring, 2)

    def quarter_rows(side, c, start=0, size=quarter):
        first = (2 * side + c) * quarter + start
        return pl.ds(pl.multiple_of(first, 16), size)

    def part_copy(c, d):
        rows = quarter_rows(parity, c)
        return to_lane(
            output_hbm.at[rows, pl.ds(pl.multiple_of(core * half, 128), half)],
            near.at[mp_count - d, rows],
            near_send.at[c, d],
            near_recv.at[c, d],
            d,
        )

    def ring_copy(c, step, side):
        rows = quarter_rows(side, c, step * (quarter // 2), quarter // 2)
        return pltpu.make_async_remote_copy(
            src_ref=near.at[1:, rows],
            dst_ref=near.at[1:, rows],
            send_sem=ring_send.at[c, step],
            recv_sem=ring_recv.at[c, step],
            device_id=(lax.rem(dp + (1 - 2 * step) * stride + dp_count, dp_count), me),
            device_id_type=MESH,
        )

    def to_sibling(index):
        if index == 0:
            source, target = near.at[0], far.at[0]
        elif index < 3:
            rows = quarter_rows(parity, index - 1)
            source, target = near.at[1:, rows], far.at[1:, rows]
        else:
            c, step = (index - 3) // 2, (index - 3) % 2
            rows = quarter_rows(1 - parity, c, step * (quarter // 2), quarter // 2)
            source, target = near.at[1:, rows], far.at[1:, rows]
        return pltpu.make_async_remote_copy(
            src_ref=source,
            dst_ref=target,
            send_sem=far_send.at[index],
            recv_sem=far_recv.at[index],
            device_id=(dp + 1 - 2 * core, me),
            device_id_type=MESH,
        )

    def pass_on(c):
        for d in range(1, mp_count):
            part_copy(c, d).wait_recv()
        for step in range(2):
            ring_copy(c, step, parity).start()
        to_sibling(1 + c).start()

    def share_ring(c):
        for step in range(2):
            ring_copy(c, step, 1 - parity).wait_recv()
            to_sibling(3 + 2 * c + step).start()

    @pl.loop(1, dp_count)
    def _(d):
        exchange(d).start()

    for c in range(2):
        for d in range(1, mp_count):
            part_copy(c, d).start()

    loads[5].wait()
    loads[6].wait()
    twice = one_hot(iota((CH, 2 * CH), 0) == iota((CH, 2 * CH), 1) % CH)
    taps = [dot(conv_first[d], twice) for d in range(3)]
    first_table[3 * N_MEL :, :] = jnp.zeros((256 - 3 * N_MEL, width), BF16)
    offset = iota((N_MEL, 2 * CH), 0) - 2 * (iota((N_MEL, 2 * CH), 1) // CH) + 1
    for n in range(MEL_HALF // 2):
        for t in range(3):
            block = jnp.zeros(offset.shape, F32)
            for d in range(3):
                block = jnp.where(offset - 4 * n == d, taps[d][t : t + 1, :], block)
            first_table[t * N_MEL : (t + 1) * N_MEL, 2 * CH * n : 2 * CH * (n + 1)] = block.astype(BF16)
    spread = one_hot(iota((CH, 4 * CH), 0) == iota((CH, 4 * CH), 1) // 4)
    sub_band = iota((CH, 4 * CH), 1) % 4
    for t in range(3):
        wide = [contract(conv_second[d, t], spread, 0, 0) for d in range(3)]
        for k in range(10):
            block = jnp.zeros((CH, 4 * CH), F32)
            for d in range(3):
                block = jnp.where(2 * sub_band + d + 1 == k, wide[d], block)
            start = k // 2 * 384 + t * 128 + k % 2 * CH
            second_table[start : start + CH, :] = block.astype(BF16)
    span = 16 * MEL_SUB
    out_row, in_row = iota((span, span), 0), iota((span, span), 1)
    source = (out_row % 64 // 4) * MEL_SUB + out_row // 64 * 4 + out_row % 4
    order = one_hot(in_row == source)
    loads[10].wait()
    for block in range(4):
        value = dot(order, raw[block * span : (block + 1) * span, :]).astype(BF16)
        for g in range(5):
            weight[256 * g + 64 * block : 256 * g + 64 * (block + 1), :] = value[64 * g : 64 * (g + 1), :]
    shifted[:, :, 3 * N_MEL :] = jnp.zeros((3, rows, 256 - 3 * N_MEL), BF16)
    hidden[:, :384] = jnp.zeros((rows, 384), BF16)

    loads[7].wait()
    loads[8].wait()
    loads[9].wait()
    loads[11].wait()
    loads[12].wait()
    loads[13].wait()
    loads[14].wait()
    arrival = arrivals[...]
    position = (dp + dp_count - arrival // capacity) % dp_count * capacity + arrival % capacity
    take = (iota((slots, per_block), 0) == position).astype(F32)
    take = jnp.transpose(take).astype(BF16)
    to_sibling(0).start()
    pass_on(0)

    @pl.loop(1, dp_count)
    def _(d):
        exchange(d).wait_recv()

    for d in range(dp_count):
        slots_rows[capacity * d : capacity * (d + 1), :] = incoming[d].astype(F32)
    windows[0] = dot(take, slots_rows[...].astype(BF16)).astype(BF16)

    last = mp_count - 1
    window_out = {
        d: to_lane(
            windows.at[0], windows.at[mp_count - d], gather_send.at[d], gather_recv.at[mp_count - d], d
        )
        for d in (1, last, 2)
    }
    for copy in window_out.values():
        copy.start()

    def wait_window(d):
        to_lane(windows.at[0], windows.at[d], gather_send.at[d], gather_recv.at[d], d).wait_recv()

    def convolve(start, stop, image):
        span = slice(start, stop)
        for t in range(3):
            first = (1 + 2 * t) * N_MEL
            shifted[t, span, : 3 * N_MEL] = image[:, first : first + 3 * N_MEL]
        for t in range(3):
            for n in range(width // 256):
                value = dot(shifted[t, span, :], first_table[:, n * 256 : (n + 1) * 256])
                value = jnp.maximum(value, 0.0).astype(BF16)
                for pair in range(2):
                    lanes = 384 * (1 + 2 * n + pair) + 128 * t
                    hidden[span, lanes : lanes + 128] = value[:, 128 * pair : 128 * (pair + 1)]
        for g in range(5):
            value = dot(hidden[span, 1536 * g : 1536 * g + 1920], second_table[...])
            features[span, 256 * g : 256 * (g + 1)] = jnp.maximum(value, 0.0).astype(BF16)

    def project(start, stop):
        span = slice(start, stop)
        for n in range(model // 256):
            embedded[span, n * 256 : (n + 1) * 256] = dot(
                features[span, :], weight[:, n * 256 : (n + 1) * 256]
            ).astype(BF16)
        gain = norm_gain[...].reshape(1, model)
        for b in range(start, stop, per_block):
            values = embedded[b : b + per_block, :].astype(F32)
            centre = values - jnp.mean(values, axis=-1, keepdims=True)
            variance = jnp.mean(centre * centre, axis=-1, keepdims=True)
            normed[b : b + per_block, :] = (centre * lax.rsqrt(variance + 1e-05) * gain).astype(BF16)
        for start in range(0, 3 * local, 256):
            lanes = slice(start, min(start + 256, 3 * local))
            projected[span, lanes] = dot(normed[span, :], attention[:, lanes]).astype(BF16)

    lower = iota((per_block, 128), 1) < HEAD_DIM
    zero = jnp.zeros((per_block, 128), BF16)

    def attend(b, target):
        d = (0, 1, last, 2)[b]
        block_ids = ids[pl.ds(lax.rem(me + d, mp_count), 1), :]
        across = jnp.broadcast_to(block_ids, (per_block, per_block))
        same = across == jnp.transpose(across)
        span = slice(b * per_block, (b + 1) * per_block)
        for pair in range(local // 128):
            lanes = slice(pair * 128, (pair + 1) * 128)
            query = projected[span, lanes]
            key = projected[span, local + pair * 128 : local + (pair + 1) * 128]
            value = projected[span, 2 * local + pair * 128 : 2 * local + (pair + 1) * 128]
            key_pair = jnp.concatenate(
                [jnp.where(lower, key, zero), jnp.where(lower, zero, key)], axis=0
            )
            value_pair = jnp.concatenate(
                [jnp.where(lower, value, zero), jnp.where(lower, zero, value)], axis=0
            )
            scores = contract(query, key_pair, 1, 1) * (1.0 / math.sqrt(HEAD_DIM))
            weights = []
            for side in range(2):
                part = jnp.where(same, scores[:, side * per_block : (side + 1) * per_block], -jnp.inf)
                largest = jnp.max(part, axis=-1, keepdims=True)
                exponent = jnp.exp(part - largest)
                total = jnp.sum(exponent, axis=-1, keepdims=True)
                weights.append((exponent / total).astype(BF16))
            target[b, :, lanes] = dot(jnp.concatenate(weights, axis=1), value_pair).astype(BF16)

    context_out = {}

    def share_contexts(d, block):
        attend(block, sending)
        context_out[d] = to_lane(
            sending.at[block],
            contexts.at[mp_count - d],
            context_send.at[d],
            context_recv.at[mp_count - d],
            d,
        )
        context_out[d].start()

    convolve(0, per_block, windows[0])
    pass_on(1)
    project(0, per_block)
    attend(0, contexts)
    wait_window(1)
    wait_window(last)
    image = jnp.concatenate([windows[1], windows[last]], axis=0)
    convolve(per_block, 3 * per_block, image)
    wait_window(2)
    project(per_block, 3 * per_block)
    share_contexts(1, 1)
    share_contexts(last, 2)
    convolve(3 * per_block, rows, windows[2])
    share_ring(0)
    project(3 * per_block, rows)
    share_ring(1)
    share_contexts(2, 3)
    for index in range(7):
        to_sibling(index).wait_recv()

    sides = [embedded[:per_block, pl.ds(pl.multiple_of(index * half, 128), half)].astype(F32) for index in (core, 1 - core)]
    for d in (0, 1, last, 2):
        if d:
            to_lane(sending.at[d], contexts.at[d], context_send.at[d], context_recv.at[d], d).wait_recv()
        for index, part in enumerate((near, far)):
            sides[index] += dot(contexts[d], part[d])
    for index, value in zip((core, 1 - core), sides):
        encoded[:, pl.ds(pl.multiple_of(index * half, 128), half)] = value.astype(BF16)

    @pl.loop(1, dp_count)
    def _(d):
        exchange(d).wait_send()

    for copy in list(window_out.values()) + list(context_out.values()):
        copy.wait_send()
    for c in range(2):
        for d in range(1, mp_count):
            part_copy(c, d).wait_send()
        for step in range(2):
            ring_copy(c, step, parity).wait_send()
    for index in range(7):
        to_sibling(index).wait_send()


def on_device(
    dp_count,
    mp_count,
    waveform,
    lengths,
    conv_first,
    conv_second,
    input_weight,
    norm_gain,
    attention_in,
    attention_out,
    send_slots,
    receive_slots,
    segment_ids,
):
    capacity = send_slots.shape[3]
    utterances = waveform.shape[2]
    per_block = receive_slots.shape[2]
    model = input_weight.shape[1]
    local = attention_in.shape[2]
    half = model // 2
    rows = mp_count * per_block
    slots = dp_count * capacity
    dma = pltpu.SemaphoreType.DMA
    operands = (
        waveform[0, 0],
        lengths[0],
        send_slots[0, :, 0, :].transpose(1, 0),
        receive_slots[0],
        conv_first.transpose(1, 2, 3, 0)[0],
        conv_second.transpose(2, 3, 0, 1),
        jnp.asarray(dft_table()),
        jnp.asarray(mel_table()),
        input_weight,
        norm_gain,
        attention_in.transpose(1, 0, 2),
        attention_out,
        segment_ids[0],
    )
    encoded = pl.pallas_call(
        functools.partial(solution_kernel, dp_count, mp_count),
        out_shape=jax.ShapeDtypeStruct((per_block, model), BF16),
        in_specs=[pl.BlockSpec(memory_space=pltpu.HBM)] * len(operands),
        out_specs=pl.BlockSpec(memory_space=VMEM),
        scratch_shapes=[
            VMEM(waveform.shape[2:], BF16),
            VMEM((1, utterances), jnp.int32),
            VMEM((capacity, dp_count), jnp.int32),
            VMEM((1, per_block), jnp.int32),
            VMEM((3, 3, CH), BF16),
            VMEM((3, 3, CH, CH), BF16),
            VMEM((4, 512, 512), BF16),
            VMEM((4, 256, WINDOW), BF16),
            VMEM((CH * MEL_SUB, model), BF16),
            VMEM((model,), F32),
            VMEM((model, 3 * local), BF16),
            VMEM((mp_count, local, half), BF16),
            VMEM((mp_count, local, half), BF16),
            VMEM((mp_count, per_block), jnp.int32),
            VMEM((256, MEL_HALF * CH), BF16),
            VMEM((30 * CH, 4 * CH), BF16),
            VMEM((CH * MEL_SUB, model), BF16),
            VMEM((utterances * SLOT_ROWS, 896), BF16),
            VMEM((slots, WINDOW), F32),
            VMEM((dp_count, capacity, WINDOW), BF16),
            VMEM((dp_count, capacity, WINDOW), BF16),
            VMEM((mp_count, per_block, WINDOW), BF16),
            VMEM((3, rows, 256), BF16),
            VMEM((rows, 384 + 3 * MEL_HALF * CH), BF16),
            VMEM((rows, CH * MEL_SUB), BF16),
            VMEM((rows, model), BF16),
            VMEM((rows, model), BF16),
            VMEM((rows, 3 * local), BF16),
            VMEM((mp_count, per_block, local), BF16),
            VMEM((mp_count, per_block, local), BF16),
            dma((15,)),
            dma((dp_count,)),
            dma((dp_count,)),
            dma((mp_count,)),
            dma((mp_count,)),
            dma((2, mp_count)),
            dma((2, mp_count)),
            dma((2, 2)),
            dma((2, 2)),
            dma((7,)),
            dma((7,)),
            dma((mp_count,)),
            dma((mp_count,)),
        ],
        compiler_params=pltpu.CompilerParams(
            vmem_limit_bytes=60 * 2**20, collective_id=0, has_side_effects=True
        ),
        name="encode",
    )(*operands)
    return encoded.reshape(1, 1, per_block, model)


def solution(mesh):
    return jax.shard_map(
        functools.partial(on_device, mesh.shape["dp"], mesh.shape["mp"]),
        mesh=mesh,
        in_specs=(
            P("dp", "mp", None, None),
            P("dp", "mp", None),
            P(),
            P(),
            P(),
            P(),
            P(None, None, "mp"),
            P("mp", None),
            P("dp", None, "mp", None),
            P("dp", "mp", None),
            P("dp", None, None),
        ),
        out_specs=P("dp", "mp", None, None),
        check_vma=False,
    )
```

```python
import functools
import math

import jax
import jax.numpy as jnp
import ml_dtypes
import numpy as np
from jax import lax
from jax.experimental import pallas as pl
from jax.experimental.pallas import tpu as pltpu
from jax.sharding import PartitionSpec as P

N_MEL = 80
N_FFT = 400
HOP = 160
HEAD_DIM = 64
SLOT_ROWS = 64
CH = 64
MEL_HALF = 40
MEL_SUB = 20
STEP = 4 * HOP
ROW = 4 * N_MEL
WINDOW = 2 * ROW
X_CHIPS = 4
MESH = pl.DeviceIdType.MESH
VMEM = pltpu.VMEM
BF16 = jnp.bfloat16
F32 = jnp.float32


def dft_table():
    position = np.arange(N_FFT)[:, None]
    harmonic = np.arange(256)[None, :]
    angles = 2.0 * math.pi * ((position * harmonic) % N_FFT) / N_FFT
    window = (0.5 - 0.5 * np.cos(2.0 * math.pi * position / N_FFT)) / math.sqrt(N_FFT)
    inside = harmonic <= N_FFT // 2
    base = np.concatenate(
        [np.where(inside, np.cos(angles), 0.0), np.where(inside, -np.sin(angles), 0.0)], axis=1
    )
    table = np.zeros((4, 512, 512))
    for r in range(4):
        table[r, 32 * r : 32 * r + N_FFT] = base * window
    return table.astype(ml_dtypes.bfloat16)


def mel_table():
    frequency = np.arange(N_FFT // 2 + 1) * (16000.0 / N_FFT)
    mel_top = 2595.0 * math.log10(1.0 + 8000.0 / 700.0)
    points = np.arange(N_MEL + 2) * (mel_top / (N_MEL + 1))
    hertz = 700.0 * (10.0 ** (points / 2595.0) - 1.0)
    lower, centre, upper = hertz[:-2], hertz[1:-1], hertz[2:]
    rising = (frequency[:, None] - lower) / (centre - lower)
    falling = (upper - frequency[:, None]) / (upper - centre)
    weights = np.maximum(0.0, np.minimum(rising, falling))
    table = np.zeros((4, 256, WINDOW))
    for r in range(4):
        for half in range(2):
            start = half * ROW + r * N_MEL
            table[r, : N_FFT // 2 + 1, start : start + N_MEL] = weights
    return table.astype(ml_dtypes.bfloat16)


def dot(a, b):
    return jnp.dot(a, b, preferred_element_type=F32)


def one_hot(condition):
    return condition.astype(F32).astype(BF16)


def iota(shape, dimension):
    return lax.broadcasted_iota(jnp.int32, shape, dimension)


def contract(a, b, dim_a, dim_b):
    return lax.dot_general(a, b, (((dim_a,), (dim_b,)), ((), ())), preferred_element_type=F32)


def solution_kernel(
    dp_count,
    mp_count,
    wave_hbm,
    lengths_hbm,
    picks_hbm,
    arrivals_hbm,
    first_hbm,
    second_hbm,
    dft_hbm,
    mel_hbm,
    weight_hbm,
    gain_hbm,
    attention_hbm,
    output_hbm,
    ids_hbm,
    encoded,
    wave,
    lengths,
    picks,
    arrivals,
    conv_first,
    conv_second,
    dft,
    mel,
    raw,
    norm_gain,
    attention,
    near,
    far,
    ids,
    first_table,
    second_table,
    weight,
    samples,
    slots_rows,
    outgoing,
    incoming,
    windows,
    shifted,
    hidden,
    features,
    embedded,
    normed,
    projected,
    sending,
    contexts,
    load_sems,
    exchange_send,
    exchange_recv,
    gather_send,
    gather_recv,
    near_send,
    near_recv,
    ring_send,
    ring_recv,
    far_send,
    far_recv,
    context_send,
    context_recv,
):
    dp, me = lax.axis_index("dp"), lax.axis_index("mp")
    core = lax.rem(dp, 2)
    capacity = picks.shape[0]
    utterances = wave.shape[0]
    frames = utterances * SLOT_ROWS
    slots = dp_count * capacity
    per_block = windows.shape[1]
    rows = mp_count * per_block
    model = weight.shape[1]
    local = attention.shape[1] // 3
    half = model // 2
    width = MEL_HALF * CH

    own_output = output_hbm.at[:, pl.ds(pl.multiple_of(core * half, 128), half)]
    plan = [
        (wave_hbm, wave),
        (dft_hbm, dft),
        (mel_hbm, mel),
        (lengths_hbm, lengths),
        (picks_hbm, picks),
        (first_hbm, conv_first),
        (second_hbm, conv_second),
        (arrivals_hbm, arrivals),
        (ids_hbm, ids),
        (gain_hbm, norm_gain),
        (weight_hbm, raw),
        (own_output, near.at[0]),
    ]
    for part in range(3):
        plan.append((attention_hbm.at[part], attention.at[:, part * local : (part + 1) * local]))
    loads = [
        pltpu.make_async_copy(source, target, load_sems.at[index])
        for index, (source, target) in enumerate(plan)
    ]
    for load in loads[:5]:
        load.start()

    barrier = pltpu.get_barrier_semaphore()

    @pl.loop(1, dp_count)
    def _(d):
        pl.semaphore_signal(
            barrier, inc=1, device_id=(lax.rem(dp + d, dp_count), me), device_id_type=MESH
        )

    for d in range(1, mp_count):
        pl.semaphore_signal(
            barrier, inc=1, device_id=(dp, lax.rem(me + d, mp_count)), device_id_type=MESH
        )

    for load in loads[5:]:
        load.start()

    loads[0].wait()
    for s in range(SLOT_ROWS):
        samples[utterances * s : utterances * (s + 1), :] = wave[:, STEP * s : STEP * s + 896]
    loads[1].wait()
    loads[2].wait()
    energy = jnp.zeros((frames, WINDOW), F32)
    for r in range(4):
        spectrum = dot(samples[:, 128 * r : 128 * r + 512], dft[r])
        power = spectrum[:, :256] * spectrum[:, :256] + spectrum[:, 256:] * spectrum[:, 256:]
        energy += dot(power.astype(BF16), mel[r])
    loads[3].wait()
    row = iota((frames, 1), 0)
    limit = jnp.broadcast_to(lengths[0:1, 0:1], (frames, 1))
    for u in range(1, utterances):
        limit = jnp.where(row % utterances == u, lengths[0:1, u : u + 1], limit)
    image = jnp.where(row // utterances < limit, jnp.log(energy + 0.01), 0.0).astype(BF16)

    loads[4].wait()
    target = (dp + iota((slots, dp_count), 0) // capacity) % dp_count
    chosen = contract(
        one_hot(iota((slots, dp_count), 1) == target), picks[...].astype(F32).astype(BF16), 1, 1
    )
    chosen = jnp.where(
        iota((slots, capacity), 1) == iota((slots, capacity), 0) % capacity, chosen, 0.0
    )
    pick = jnp.sum(chosen, axis=1, keepdims=True).astype(jnp.int32)
    place = jnp.where(pick < 0, -SLOT_ROWS, pick % SLOT_ROWS * utterances + pick // SLOT_ROWS)
    column = iota((slots, frames), 1)
    own = dot(one_hot(column == place), image)
    earlier = dot(one_hot(column == place - utterances), image)
    slots_rows[...] = jnp.where(iota(own.shape, 1) < ROW, earlier, own)
    for d in range(dp_count):
        slab = slots_rows[capacity * d : capacity * (d + 1), :].astype(BF16)
        if d == 0:
            incoming[0] = slab
        else:
            outgoing[d] = slab

    pl.semaphore_wait(barrier, dp_count - 1 + mp_count - 1)

    def exchange(d):
        return pltpu.make_async_remote_copy(
            src_ref=outgoing.at[d],
            dst_ref=incoming.at[d],
            send_sem=exchange_send.at[d],
            recv_sem=exchange_recv.at[d],
            device_id=(lax.rem(dp + d, dp_count), me),
            device_id_type=MESH,
        )

    def to_lane(source, target, send_sem, recv_sem, d):
        return pltpu.make_async_remote_copy(
            src_ref=source,
            dst_ref=target,
            send_sem=send_sem,
            recv_sem=recv_sem,
            device_id=(dp, lax.rem(me + d, mp_count)),
            device_id_type=MESH,
        )

    stride = dp_count // X_CHIPS
    ring = dp // stride
    quarter = local // 4
    parity = lax.rem(ring, 2)

    def quarter_rows(side, c, start=0, size=quarter):
        first = (2 * side + c) * quarter + start
        return pl.ds(pl.multiple_of(first, 16), size)

    def part_copy(c, d):
        rows = quarter_rows(parity, c)
        return to_lane(
            output_hbm.at[rows, pl.ds(pl.multiple_of(core * half, 128), half)],
            near.at[mp_count - d, rows],
            near_send.at[c, d],
            near_recv.at[c, d],
            d,
        )

    def ring_copy(c, step, side):
        rows = quarter_rows(side, c, step * (quarter // 2), quarter // 2)
        return pltpu.make_async_remote_copy(
            src_ref=near.at[1:, rows],
            dst_ref=near.at[1:, rows],
            send_sem=ring_send.at[c, step],
            recv_sem=ring_recv.at[c, step],
            device_id=(lax.rem(dp + (1 - 2 * step) * stride + dp_count, dp_count), me),
            device_id_type=MESH,
        )

    def to_sibling(index):
        if index == 0:
            source, target = near.at[0], far.at[0]
        elif index < 3:
            rows = quarter_rows(parity, index - 1)
            source, target = near.at[1:, rows], far.at[1:, rows]
        else:
            c, step = (index - 3) // 2, (index - 3) % 2
            rows = quarter_rows(1 - parity, c, step * (quarter // 2), quarter // 2)
            source, target = near.at[1:, rows], far.at[1:, rows]
        return pltpu.make_async_remote_copy(
            src_ref=source,
            dst_ref=target,
            send_sem=far_send.at[index],
            recv_sem=far_recv.at[index],
            device_id=(dp + 1 - 2 * core, me),
            device_id_type=MESH,
        )

    def pass_on(c):
        for d in range(1, mp_count):
            part_copy(c, d).wait_recv()
        for step in range(2):
            ring_copy(c, step, parity).start()
        to_sibling(1 + c).start()

    def share_ring(c):
        for step in range(2):
            ring_copy(c, step, 1 - parity).wait_recv()
            to_sibling(3 + 2 * c + step).start()

    @pl.loop(1, dp_count)
    def _(d):
        exchange(d).start()

    for d in range(1, mp_count):
        part_copy(0, d).start()

    loads[5].wait()
    loads[6].wait()
    twice = one_hot(iota((CH, 2 * CH), 0) == iota((CH, 2 * CH), 1) % CH)
    taps = [dot(conv_first[d], twice) for d in range(3)]
    first_table[3 * N_MEL :, :] = jnp.zeros((256 - 3 * N_MEL, width), BF16)
    offset = iota((N_MEL, 2 * CH), 0) - 2 * (iota((N_MEL, 2 * CH), 1) // CH) + 1
    for n in range(MEL_HALF // 2):
        for t in range(3):
            block = jnp.zeros(offset.shape, F32)
            for d in range(3):
                block = jnp.where(offset - 4 * n == d, taps[d][t : t + 1, :], block)
            first_table[t * N_MEL : (t + 1) * N_MEL, 2 * CH * n : 2 * CH * (n + 1)] = block.astype(BF16)
    spread = one_hot(iota((CH, 4 * CH), 0) == iota((CH, 4 * CH), 1) // 4)
    sub_band = iota((CH, 4 * CH), 1) % 4
    for t in range(3):
        wide = [contract(conv_second[d, t], spread, 0, 0) for d in range(3)]
        for k in range(10):
            block = jnp.zeros((CH, 4 * CH), F32)
            for d in range(3):
                block = jnp.where(2 * sub_band + d + 1 == k, wide[d], block)
            start = k // 2 * 384 + t * 128 + k % 2 * CH
            second_table[start : start + CH, :] = block.astype(BF16)
    span = 16 * MEL_SUB
    out_row, in_row = iota((span, span), 0), iota((span, span), 1)
    source = (out_row % 64 // 4) * MEL_SUB + out_row // 64 * 4 + out_row % 4
    order = one_hot(in_row == source)
    loads[10].wait()
    for block in range(4):
        value = dot(order, raw[block * span : (block + 1) * span, :]).astype(BF16)
        for g in range(5):
            weight[256 * g + 64 * block : 256 * g + 64 * (block + 1), :] = value[64 * g : 64 * (g + 1), :]
    for d in range(1, mp_count):
        part_copy(1, d).start()
    shifted[:, :, 3 * N_MEL :] = jnp.zeros((3, rows, 256 - 3 * N_MEL), BF16)
    hidden[:, :384] = jnp.zeros((rows, 384), BF16)

    loads[7].wait()
    loads[8].wait()
    loads[9].wait()
    loads[11].wait()
    loads[12].wait()
    loads[13].wait()
    loads[14].wait()
    arrival = arrivals[...]
    position = (dp + dp_count - arrival // capacity) % dp_count * capacity + arrival % capacity
    take = (iota((slots, per_block), 0) == position).astype(F32)
    take = jnp.transpose(take).astype(BF16)
    to_sibling(0).start()
    pass_on(0)

    @pl.loop(1, dp_count)
    def _(d):
        exchange(d).wait_recv()

    for d in range(dp_count):
        slots_rows[capacity * d : capacity * (d + 1), :] = incoming[d].astype(F32)
    windows[0] = dot(take, slots_rows[...].astype(BF16)).astype(BF16)

    last = mp_count - 1
    window_out = {
        d: to_lane(
            windows.at[0], windows.at[mp_count - d], gather_send.at[d], gather_recv.at[mp_count - d], d
        )
        for d in (1, last, 2)
    }
    window_out[1].start()
    window_out[last].start()

    def wait_window(d):
        to_lane(windows.at[0], windows.at[d], gather_send.at[d], gather_recv.at[d], d).wait_recv()

    def convolve(start, stop, image):
        span = slice(start, stop)
        for t in range(3):
            first = (1 + 2 * t) * N_MEL
            shifted[t, span, : 3 * N_MEL] = image[:, first : first + 3 * N_MEL]
        for t in range(3):
            for n in range(width // 256):
                value = dot(shifted[t, span, :], first_table[:, n * 256 : (n + 1) * 256])
                value = jnp.maximum(value, 0.0).astype(BF16)
                for pair in range(2):
                    lanes = 384 * (1 + 2 * n + pair) + 128 * t
                    hidden[span, lanes : lanes + 128] = value[:, 128 * pair : 128 * (pair + 1)]
        for g in range(5):
            value = dot(hidden[span, 1536 * g : 1536 * g + 1920], second_table[...])
            features[span, 256 * g : 256 * (g + 1)] = jnp.maximum(value, 0.0).astype(BF16)

    def project(start, stop):
        span = slice(start, stop)
        for n in range(model // 256):
            embedded[span, n * 256 : (n + 1) * 256] = dot(
                features[span, :], weight[:, n * 256 : (n + 1) * 256]
            ).astype(BF16)
        gain = norm_gain[...].reshape(1, model)
        for b in range(start, stop, per_block):
            values = embedded[b : b + per_block, :].astype(F32)
            centre = values - jnp.mean(values, axis=-1, keepdims=True)
            variance = jnp.mean(centre * centre, axis=-1, keepdims=True)
            normed[b : b + per_block, :] = (centre * lax.rsqrt(variance + 1e-05) * gain).astype(BF16)
        for start in range(0, 3 * local, 256):
            lanes = slice(start, min(start + 256, 3 * local))
            projected[span, lanes] = dot(normed[span, :], attention[:, lanes]).astype(BF16)

    lower = iota((per_block, 128), 1) < HEAD_DIM
    zero = jnp.zeros((per_block, 128), BF16)

    def attend(b, target):
        d = (0, 1, last, 2)[b]
        block_ids = ids[pl.ds(lax.rem(me + d, mp_count), 1), :]
        across = jnp.broadcast_to(block_ids, (per_block, per_block))
        same = across == jnp.transpose(across)
        span = slice(b * per_block, (b + 1) * per_block)
        for pair in range(local // 128):
            lanes = slice(pair * 128, (pair + 1) * 128)
            query = projected[span, lanes]
            key = projected[span, local + pair * 128 : local + (pair + 1) * 128]
            value = projected[span, 2 * local + pair * 128 : 2 * local + (pair + 1) * 128]
            key_pair = jnp.concatenate(
                [jnp.where(lower, key, zero), jnp.where(lower, zero, key)], axis=0
            )
            value_pair = jnp.concatenate(
                [jnp.where(lower, value, zero), jnp.where(lower, zero, value)], axis=0
            )
            scores = contract(query, key_pair, 1, 1) * (1.0 / math.sqrt(HEAD_DIM))
            weights = []
            for side in range(2):
                part = jnp.where(same, scores[:, side * per_block : (side + 1) * per_block], -jnp.inf)
                largest = jnp.max(part, axis=-1, keepdims=True)
                exponent = jnp.exp(part - largest)
                total = jnp.sum(exponent, axis=-1, keepdims=True)
                weights.append((exponent / total).astype(BF16))
            target[b, :, lanes] = dot(jnp.concatenate(weights, axis=1), value_pair).astype(BF16)

    context_out = {}

    def share_contexts(d, block):
        attend(block, sending)
        context_out[d] = to_lane(
            sending.at[block],
            contexts.at[mp_count - d],
            context_send.at[d],
            context_recv.at[mp_count - d],
            d,
        )
        context_out[d].start()

    convolve(0, per_block, windows[0])
    pass_on(1)
    project(0, per_block)
    attend(0, contexts)
    wait_window(1)
    wait_window(last)
    window_out[2].start()
    image = jnp.concatenate([windows[1], windows[last]], axis=0)
    convolve(per_block, 3 * per_block, image)
    project(per_block, 3 * per_block)
    share_contexts(1, 1)
    share_contexts(last, 2)
    wait_window(2)
    convolve(3 * per_block, rows, windows[2])
    share_ring(0)
    project(3 * per_block, rows)
    share_ring(1)
    share_contexts(2, 3)
    for index in range(7):
        to_sibling(index).wait_recv()

    sides = [embedded[:per_block, pl.ds(pl.multiple_of(index * half, 128), half)].astype(F32) for index in (core, 1 - core)]
    for d in (0, 1, last, 2):
        if d:
            to_lane(sending.at[d], contexts.at[d], context_send.at[d], context_recv.at[d], d).wait_recv()
        for index, part in enumerate((near, far)):
            sides[index] += dot(contexts[d], part[d])
    for index, value in zip((core, 1 - core), sides):
        encoded[:, pl.ds(pl.multiple_of(index * half, 128), half)] = value.astype(BF16)

    @pl.loop(1, dp_count)
    def _(d):
        exchange(d).wait_send()

    for copy in list(window_out.values()) + list(context_out.values()):
        copy.wait_send()
    for c in range(2):
        for d in range(1, mp_count):
            part_copy(c, d).wait_send()
        for step in range(2):
            ring_copy(c, step, parity).wait_send()
    for index in range(7):
        to_sibling(index).wait_send()


def on_device(
    dp_count,
    mp_count,
    waveform,
    lengths,
    conv_first,
    conv_second,
    input_weight,
    norm_gain,
    attention_in,
    attention_out,
    send_slots,
    receive_slots,
    segment_ids,
):
    capacity = send_slots.shape[3]
    utterances = waveform.shape[2]
    per_block = receive_slots.shape[2]
    model = input_weight.shape[1]
    local = attention_in.shape[2]
    half = model // 2
    rows = mp_count * per_block
    slots = dp_count * capacity
    dma = pltpu.SemaphoreType.DMA
    operands = (
        waveform[0, 0],
        lengths[0],
        send_slots[0, :, 0, :].transpose(1, 0),
        receive_slots[0],
        conv_first.transpose(1, 2, 3, 0)[0],
        conv_second.transpose(2, 3, 0, 1),
        jnp.asarray(dft_table()),
        jnp.asarray(mel_table()),
        input_weight,
        norm_gain,
        attention_in.transpose(1, 0, 2),
        attention_out,
        segment_ids[0],
    )
    encoded = pl.pallas_call(
        functools.partial(solution_kernel, dp_count, mp_count),
        out_shape=jax.ShapeDtypeStruct((per_block, model), BF16),
        in_specs=[pl.BlockSpec(memory_space=pltpu.HBM)] * len(operands),
        out_specs=pl.BlockSpec(memory_space=VMEM),
        scratch_shapes=[
            VMEM(waveform.shape[2:], BF16),
            VMEM((1, utterances), jnp.int32),
            VMEM((capacity, dp_count), jnp.int32),
            VMEM((1, per_block), jnp.int32),
            VMEM((3, 3, CH), BF16),
            VMEM((3, 3, CH, CH), BF16),
            VMEM((4, 512, 512), BF16),
            VMEM((4, 256, WINDOW), BF16),
            VMEM((CH * MEL_SUB, model), BF16),
            VMEM((model,), F32),
            VMEM((model, 3 * local), BF16),
            VMEM((mp_count, local, half), BF16),
            VMEM((mp_count, local, half), BF16),
            VMEM((mp_count, per_block), jnp.int32),
            VMEM((256, MEL_HALF * CH), BF16),
            VMEM((30 * CH, 4 * CH), BF16),
            VMEM((CH * MEL_SUB, model), BF16),
            VMEM((utterances * SLOT_ROWS, 896), BF16),
            VMEM((slots, WINDOW), F32),
            VMEM((dp_count, capacity, WINDOW), BF16),
            VMEM((dp_count, capacity, WINDOW), BF16),
            VMEM((mp_count, per_block, WINDOW), BF16),
            VMEM((3, rows, 256), BF16),
            VMEM((rows, 384 + 3 * MEL_HALF * CH), BF16),
            VMEM((rows, CH * MEL_SUB), BF16),
            VMEM((rows, model), BF16),
            VMEM((rows, model), BF16),
            VMEM((rows, 3 * local), BF16),
            VMEM((mp_count, per_block, local), BF16),
            VMEM((mp_count, per_block, local), BF16),
            dma((15,)),
            dma((dp_count,)),
            dma((dp_count,)),
            dma((mp_count,)),
            dma((mp_count,)),
            dma((2, mp_count)),
            dma((2, mp_count)),
            dma((2, 2)),
            dma((2, 2)),
            dma((7,)),
            dma((7,)),
            dma((mp_count,)),
            dma((mp_count,)),
        ],
        compiler_params=pltpu.CompilerParams(
            vmem_limit_bytes=60 * 2**20, collective_id=0, has_side_effects=True
        ),
        name="encode",
    )(*operands)
    return encoded.reshape(1, 1, per_block, model)


def solution(mesh):
    return jax.shard_map(
        functools.partial(on_device, mesh.shape["dp"], mesh.shape["mp"]),
        mesh=mesh,
        in_specs=(
            P("dp", "mp", None, None),
            P("dp", "mp", None),
            P(),
            P(),
            P(),
            P(),
            P(None, None, "mp"),
            P("mp", None),
            P("dp", None, "mp", None),
            P("dp", "mp", None),
            P("dp", None, None),
        ),
        out_specs=P("dp", "mp", None, None),
        check_vma=False,
    )
```

```python
import functools
import math

import jax
import jax.numpy as jnp
import ml_dtypes
import numpy as np
from jax import lax
from jax.experimental import pallas as pl
from jax.experimental.pallas import tpu as pltpu
from jax.sharding import PartitionSpec as P

N_MEL = 80
N_FFT = 400
HOP = 160
HEAD_DIM = 64
SLOT_ROWS = 64
CH = 64
MEL_HALF = 40
MEL_SUB = 20
STEP = 4 * HOP
ROW = 4 * N_MEL
WINDOW = 2 * ROW
X_CHIPS = 4
MESH = pl.DeviceIdType.MESH
VMEM = pltpu.VMEM
BF16 = jnp.bfloat16
F32 = jnp.float32


def dft_table():
    position = np.arange(N_FFT)[:, None]
    harmonic = np.arange(256)[None, :]
    angles = 2.0 * math.pi * ((position * harmonic) % N_FFT) / N_FFT
    window = (0.5 - 0.5 * np.cos(2.0 * math.pi * position / N_FFT)) / math.sqrt(N_FFT)
    inside = harmonic <= N_FFT // 2
    base = np.concatenate(
        [np.where(inside, np.cos(angles), 0.0), np.where(inside, -np.sin(angles), 0.0)], axis=1
    )
    table = np.zeros((4, 512, 512))
    for r in range(4):
        table[r, 32 * r : 32 * r + N_FFT] = base * window
    return table.astype(ml_dtypes.bfloat16)


def mel_table():
    frequency = np.arange(N_FFT // 2 + 1) * (16000.0 / N_FFT)
    mel_top = 2595.0 * math.log10(1.0 + 8000.0 / 700.0)
    points = np.arange(N_MEL + 2) * (mel_top / (N_MEL + 1))
    hertz = 700.0 * (10.0 ** (points / 2595.0) - 1.0)
    lower, centre, upper = hertz[:-2], hertz[1:-1], hertz[2:]
    rising = (frequency[:, None] - lower) / (centre - lower)
    falling = (upper - frequency[:, None]) / (upper - centre)
    weights = np.maximum(0.0, np.minimum(rising, falling))
    table = np.zeros((4, 256, WINDOW))
    for r in range(4):
        for half in range(2):
            start = half * ROW + r * N_MEL
            table[r, : N_FFT // 2 + 1, start : start + N_MEL] = weights
    return table.astype(ml_dtypes.bfloat16)


def dot(a, b):
    return jnp.dot(a, b, preferred_element_type=F32)


def one_hot(condition):
    return condition.astype(F32).astype(BF16)


def iota(shape, dimension):
    return lax.broadcasted_iota(jnp.int32, shape, dimension)


def contract(a, b, dim_a, dim_b):
    return lax.dot_general(a, b, (((dim_a,), (dim_b,)), ((), ())), preferred_element_type=F32)


def solution_kernel(
    dp_count,
    mp_count,
    wave_hbm,
    lengths_hbm,
    picks_hbm,
    arrivals_hbm,
    first_hbm,
    second_hbm,
    dft_hbm,
    mel_hbm,
    weight_hbm,
    gain_hbm,
    attention_hbm,
    output_hbm,
    ids_hbm,
    encoded,
    wave,
    lengths,
    picks,
    arrivals,
    conv_first,
    conv_second,
    dft,
    mel,
    raw,
    norm_gain,
    attention,
    near,
    far,
    ids,
    first_table,
    second_table,
    weight,
    samples,
    slots_rows,
    outgoing,
    incoming,
    windows,
    shifted,
    hidden,
    features,
    embedded,
    normed,
    projected,
    sending,
    contexts,
    load_sems,
    exchange_send,
    exchange_recv,
    gather_send,
    gather_recv,
    near_send,
    near_recv,
    ring_send,
    ring_recv,
    far_send,
    far_recv,
    context_send,
    context_recv,
):
    dp, me = lax.axis_index("dp"), lax.axis_index("mp")
    core = lax.rem(dp, 2)
    capacity = picks.shape[0]
    utterances = wave.shape[0]
    frames = utterances * SLOT_ROWS
    slots = dp_count * capacity
    per_block = windows.shape[1]
    rows = mp_count * per_block
    model = weight.shape[1]
    local = attention.shape[1] // 3
    half = model // 2
    width = MEL_HALF * CH

    own_output = output_hbm.at[:, pl.ds(pl.multiple_of(core * half, 128), half)]
    plan = [
        (wave_hbm, wave),
        (dft_hbm, dft),
        (mel_hbm, mel),
        (lengths_hbm, lengths),
        (picks_hbm, picks),
        (first_hbm, conv_first),
        (second_hbm, conv_second),
        (arrivals_hbm, arrivals),
        (ids_hbm, ids),
        (gain_hbm, norm_gain),
        (weight_hbm, raw),
        (own_output, near.at[0]),
    ]
    for part in range(3):
        plan.append((attention_hbm.at[part], attention.at[:, part * local : (part + 1) * local]))
    loads = [
        pltpu.make_async_copy(source, target, load_sems.at[index])
        for index, (source, target) in enumerate(plan)
    ]
    for load in loads[:5]:
        load.start()

    barrier = pltpu.get_barrier_semaphore()

    @pl.loop(1, dp_count)
    def _(d):
        pl.semaphore_signal(
            barrier, inc=1, device_id=(lax.rem(dp + d, dp_count), me), device_id_type=MESH
        )

    for d in range(1, mp_count):
        pl.semaphore_signal(
            barrier, inc=1, device_id=(dp, lax.rem(me + d, mp_count)), device_id_type=MESH
        )

    for load in loads[5:]:
        load.start()

    loads[0].wait()
    for s in range(SLOT_ROWS):
        samples[utterances * s : utterances * (s + 1), :] = wave[:, STEP * s : STEP * s + 896]
    loads[1].wait()
    loads[2].wait()
    energy = jnp.zeros((frames, WINDOW), F32)
    for r in range(4):
        spectrum = dot(samples[:, 128 * r : 128 * r + 512], dft[r])
        power = spectrum[:, :256] * spectrum[:, :256] + spectrum[:, 256:] * spectrum[:, 256:]
        energy += dot(power.astype(BF16), mel[r])
    loads[3].wait()
    row = iota((frames, 1), 0)
    limit = jnp.broadcast_to(lengths[0:1, 0:1], (frames, 1))
    for u in range(1, utterances):
        limit = jnp.where(row % utterances == u, lengths[0:1, u : u + 1], limit)
    image = jnp.where(row // utterances < limit, jnp.log(energy + 0.01), 0.0).astype(BF16)

    loads[4].wait()
    target = (dp + iota((slots, dp_count), 0) // capacity) % dp_count
    chosen = contract(
        one_hot(iota((slots, dp_count), 1) == target), picks[...].astype(F32).astype(BF16), 1, 1
    )
    chosen = jnp.where(
        iota((slots, capacity), 1) == iota((slots, capacity), 0) % capacity, chosen, 0.0
    )
    pick = jnp.sum(chosen, axis=1, keepdims=True).astype(jnp.int32)
    place = jnp.where(pick < 0, -SLOT_ROWS, pick % SLOT_ROWS * utterances + pick // SLOT_ROWS)
    column = iota((slots, frames), 1)
    own = dot(one_hot(column == place), image)
    earlier = dot(one_hot(column == place - utterances), image)
    slots_rows[...] = jnp.where(iota(own.shape, 1) < ROW, earlier, own)
    for d in range(dp_count):
        slab = slots_rows[capacity * d : capacity * (d + 1), :].astype(BF16)
        if d == 0:
            incoming[0] = slab
        else:
            outgoing[d] = slab

    pl.semaphore_wait(barrier, dp_count - 1 + mp_count - 1)

    def exchange(slab, d):
        return pltpu.make_async_remote_copy(
            src_ref=outgoing.at[slab],
            dst_ref=incoming.at[slab],
            send_sem=exchange_send,
            recv_sem=exchange_recv,
            device_id=(lax.rem(dp + d, dp_count), me),
            device_id_type=MESH,
        )

    def to_lane(source, target, send_sem, recv_sem, d):
        return pltpu.make_async_remote_copy(
            src_ref=source,
            dst_ref=target,
            send_sem=send_sem,
            recv_sem=recv_sem,
            device_id=(dp, lax.rem(me + d, mp_count)),
            device_id_type=MESH,
        )

    stride = dp_count // X_CHIPS
    ring = dp // stride
    quarter = local // 4
    parity = lax.rem(ring, 2)

    def quarter_rows(side, c, start=0, size=quarter):
        first = (2 * side + c) * quarter + start
        return pl.ds(pl.multiple_of(first, 16), size)

    def part_copy(c, d):
        rows = quarter_rows(parity, c)
        return to_lane(
            output_hbm.at[rows, pl.ds(pl.multiple_of(core * half, 128), half)],
            near.at[mp_count - d, rows],
            near_send.at[c, d],
            near_recv.at[c, d],
            d,
        )

    def ring_copy(c, step, side):
        rows = quarter_rows(side, c, step * (quarter // 2), quarter // 2)
        return pltpu.make_async_remote_copy(
            src_ref=near.at[1:, rows],
            dst_ref=near.at[1:, rows],
            send_sem=ring_send.at[c, step],
            recv_sem=ring_recv.at[c, step],
            device_id=(lax.rem(dp + (1 - 2 * step) * stride + dp_count, dp_count), me),
            device_id_type=MESH,
        )

    def to_sibling(index):
        if index == 0:
            source, target = near.at[0], far.at[0]
        elif index < 3:
            rows = quarter_rows(parity, index - 1)
            source, target = near.at[1:, rows], far.at[1:, rows]
        else:
            c, step = (index - 3) // 2, (index - 3) % 2
            rows = quarter_rows(1 - parity, c, step * (quarter // 2), quarter // 2)
            source, target = near.at[1:, rows], far.at[1:, rows]
        return pltpu.make_async_remote_copy(
            src_ref=source,
            dst_ref=target,
            send_sem=far_send.at[index],
            recv_sem=far_recv.at[index],
            device_id=(dp + 1 - 2 * core, me),
            device_id_type=MESH,
        )

    def pass_on(c):
        for d in range(1, mp_count):
            part_copy(c, d).wait_recv()
        for step in range(2):
            ring_copy(c, step, parity).start()
        to_sibling(1 + c).start()

    def share_ring(c):
        for step in range(2):
            ring_copy(c, step, 1 - parity).wait_recv()
            to_sibling(3 + 2 * c + step).start()

    @pl.loop(1, dp_count)
    def _(d):
        exchange(d, d).start()

    for d in range(1, mp_count):
        part_copy(0, d).start()

    loads[5].wait()
    loads[6].wait()
    twice = one_hot(iota((CH, 2 * CH), 0) == iota((CH, 2 * CH), 1) % CH)
    taps = [dot(conv_first[d], twice) for d in range(3)]
    first_table[3 * N_MEL :, :] = jnp.zeros((256 - 3 * N_MEL, width), BF16)
    offset = iota((N_MEL, 2 * CH), 0) - 2 * (iota((N_MEL, 2 * CH), 1) // CH) + 1
    for n in range(MEL_HALF // 2):
        for t in range(3):
            block = jnp.zeros(offset.shape, F32)
            for d in range(3):
                block = jnp.where(offset - 4 * n == d, taps[d][t : t + 1, :], block)
            first_table[t * N_MEL : (t + 1) * N_MEL, 2 * CH * n : 2 * CH * (n + 1)] = block.astype(BF16)
    spread = one_hot(iota((CH, 4 * CH), 0) == iota((CH, 4 * CH), 1) // 4)
    sub_band = iota((CH, 4 * CH), 1) % 4
    for t in range(3):
        wide = [contract(conv_second[d, t], spread, 0, 0) for d in range(3)]
        for k in range(10):
            block = jnp.zeros((CH, 4 * CH), F32)
            for d in range(3):
                block = jnp.where(2 * sub_band + d + 1 == k, wide[d], block)
            start = k // 2 * 384 + t * 128 + k % 2 * CH
            second_table[start : start + CH, :] = block.astype(BF16)
    span = 16 * MEL_SUB
    out_row, in_row = iota((span, span), 0), iota((span, span), 1)
    source = (out_row % 64 // 4) * MEL_SUB + out_row // 64 * 4 + out_row % 4
    order = one_hot(in_row == source)
    loads[10].wait()
    for block in range(4):
        value = dot(order, raw[block * span : (block + 1) * span, :]).astype(BF16)
        for g in range(5):
            weight[256 * g + 64 * block : 256 * g + 64 * (block + 1), :] = value[64 * g : 64 * (g + 1), :]
    for d in range(1, mp_count):
        part_copy(1, d).start()
    shifted[:, :, 3 * N_MEL :] = jnp.zeros((3, rows, 256 - 3 * N_MEL), BF16)
    hidden[:, :384] = jnp.zeros((rows, 384), BF16)

    loads[7].wait()
    loads[8].wait()
    loads[9].wait()
    loads[11].wait()
    loads[12].wait()
    loads[13].wait()
    loads[14].wait()
    arrival = arrivals[...]
    position = (dp + dp_count - arrival // capacity) % dp_count * capacity + arrival % capacity
    take = (iota((slots, per_block), 0) == position).astype(F32)
    take = jnp.transpose(take).astype(BF16)
    to_sibling(0).start()
    pass_on(0)

    all_slabs = exchange(pl.ds(1, dp_count - 1), 1)
    all_slabs.wait_recv()
    for d in range(dp_count):
        slots_rows[capacity * d : capacity * (d + 1), :] = incoming[d].astype(F32)
    windows[0] = dot(take, slots_rows[...].astype(BF16)).astype(BF16)

    last = mp_count - 1
    window_out = {
        d: to_lane(
            windows.at[0], windows.at[mp_count - d], gather_send.at[d], gather_recv.at[mp_count - d], d
        )
        for d in (1, last, 2)
    }
    window_out[1].start()
    window_out[last].start()

    def wait_window(d):
        to_lane(windows.at[0], windows.at[d], gather_send.at[d], gather_recv.at[d], d).wait_recv()

    def convolve(start, stop, image):
        span = slice(start, stop)
        for t in range(3):
            first = (1 + 2 * t) * N_MEL
            shifted[t, span, : 3 * N_MEL] = image[:, first : first + 3 * N_MEL]
        for t in range(3):
            for n in range(width // 256):
                value = dot(shifted[t, span, :], first_table[:, n * 256 : (n + 1) * 256])
                value = jnp.maximum(value, 0.0).astype(BF16)
                for pair in range(2):
                    lanes = 384 * (1 + 2 * n + pair) + 128 * t
                    hidden[span, lanes : lanes + 128] = value[:, 128 * pair : 128 * (pair + 1)]
        for g in range(5):
            value = dot(hidden[span, 1536 * g : 1536 * g + 1920], second_table[...])
            features[span, 256 * g : 256 * (g + 1)] = jnp.maximum(value, 0.0).astype(BF16)

    def project(start, stop):
        span = slice(start, stop)
        for n in range(model // 256):
            embedded[span, n * 256 : (n + 1) * 256] = dot(
                features[span, :], weight[:, n * 256 : (n + 1) * 256]
            ).astype(BF16)
        gain = norm_gain[...].reshape(1, model)
        for b in range(start, stop, per_block):
            values = embedded[b : b + per_block, :].astype(F32)
            centre = values - jnp.mean(values, axis=-1, keepdims=True)
            variance = jnp.mean(centre * centre, axis=-1, keepdims=True)
            normed[b : b + per_block, :] = (centre * lax.rsqrt(variance + 1e-05) * gain).astype(BF16)
        for start in range(0, 3 * local, 256):
            lanes = slice(start, min(start + 256, 3 * local))
            projected[span, lanes] = dot(normed[span, :], attention[:, lanes]).astype(BF16)

    lower = iota((per_block, 128), 1) < HEAD_DIM
    zero = jnp.zeros((per_block, 128), BF16)

    def attend(b, target):
        d = (0, 1, last, 2)[b]
        block_ids = ids[pl.ds(lax.rem(me + d, mp_count), 1), :]
        across = jnp.broadcast_to(block_ids, (per_block, per_block))
        same = across == jnp.transpose(across)
        span = slice(b * per_block, (b + 1) * per_block)
        for pair in range(local // 128):
            lanes = slice(pair * 128, (pair + 1) * 128)
            query = projected[span, lanes]
            key = projected[span, local + pair * 128 : local + (pair + 1) * 128]
            value = projected[span, 2 * local + pair * 128 : 2 * local + (pair + 1) * 128]
            key_pair = jnp.concatenate(
                [jnp.where(lower, key, zero), jnp.where(lower, zero, key)], axis=0
            )
            value_pair = jnp.concatenate(
                [jnp.where(lower, value, zero), jnp.where(lower, zero, value)], axis=0
            )
            scores = contract(query, key_pair, 1, 1) * (1.0 / math.sqrt(HEAD_DIM))
            weights = []
            for side in range(2):
                part = jnp.where(same, scores[:, side * per_block : (side + 1) * per_block], -jnp.inf)
                largest = jnp.max(part, axis=-1, keepdims=True)
                exponent = jnp.exp(part - largest)
                total = jnp.sum(exponent, axis=-1, keepdims=True)
                weights.append((exponent / total).astype(BF16))
            target[b, :, lanes] = dot(jnp.concatenate(weights, axis=1), value_pair).astype(BF16)

    context_out = {}

    def share_contexts(d, block):
        attend(block, sending)
        context_out[d] = to_lane(
            sending.at[block],
            contexts.at[mp_count - d],
            context_send.at[d],
            context_recv.at[mp_count - d],
            d,
        )
        context_out[d].start()

    convolve(0, per_block, windows[0])
    pass_on(1)
    project(0, per_block)
    attend(0, contexts)
    all_slabs.wait_send()
    for c in range(2):
        for d in range(1, mp_count):
            part_copy(c, d).wait_send()
    wait_window(1)
    wait_window(last)
    window_out[2].start()
    image = jnp.concatenate([windows[1], windows[last]], axis=0)
    convolve(per_block, 3 * per_block, image)
    project(per_block, 3 * per_block)
    share_contexts(1, 1)
    share_contexts(last, 2)
    wait_window(2)
    convolve(3 * per_block, rows, windows[2])
    share_ring(0)
    project(3 * per_block, rows)
    share_ring(1)
    share_contexts(2, 3)
    for copy in list(window_out.values()) + [context_out[1], context_out[last]]:
        copy.wait_send()
    for c in range(2):
        for step in range(2):
            ring_copy(c, step, parity).wait_send()
    for index in range(7):
        to_sibling(index).wait_send()
    for index in range(7):
        to_sibling(index).wait_recv()

    sides = [embedded[:per_block, pl.ds(pl.multiple_of(index * half, 128), half)].astype(F32) for index in (core, 1 - core)]
    for d in (0, 1, last, 2):
        if d:
            to_lane(sending.at[d], contexts.at[d], context_send.at[d], context_recv.at[d], d).wait_recv()
        for index, part in enumerate((near, far)):
            sides[index] += dot(contexts[d], part[d])
    for index, value in zip((core, 1 - core), sides):
        encoded[:, pl.ds(pl.multiple_of(index * half, 128), half)] = value.astype(BF16)

    context_out[2].wait_send()


def on_device(
    dp_count,
    mp_count,
    waveform,
    lengths,
    conv_first,
    conv_second,
    input_weight,
    norm_gain,
    attention_in,
    attention_out,
    send_slots,
    receive_slots,
    segment_ids,
):
    capacity = send_slots.shape[3]
    utterances = waveform.shape[2]
    per_block = receive_slots.shape[2]
    model = input_weight.shape[1]
    local = attention_in.shape[2]
    half = model // 2
    rows = mp_count * per_block
    slots = dp_count * capacity
    dma = pltpu.SemaphoreType.DMA
    operands = (
        waveform[0, 0],
        lengths[0],
        send_slots[0, :, 0, :].transpose(1, 0),
        receive_slots[0],
        conv_first.transpose(1, 2, 3, 0)[0],
        conv_second.transpose(2, 3, 0, 1),
        jnp.asarray(dft_table()),
        jnp.asarray(mel_table()),
        input_weight,
        norm_gain,
        attention_in.transpose(1, 0, 2),
        attention_out,
        segment_ids[0],
    )
    encoded = pl.pallas_call(
        functools.partial(solution_kernel, dp_count, mp_count),
        out_shape=jax.ShapeDtypeStruct((per_block, model), BF16),
        in_specs=[pl.BlockSpec(memory_space=pltpu.HBM)] * len(operands),
        out_specs=pl.BlockSpec(memory_space=VMEM),
        scratch_shapes=[
            VMEM(waveform.shape[2:], BF16),
            VMEM((1, utterances), jnp.int32),
            VMEM((capacity, dp_count), jnp.int32),
            VMEM((1, per_block), jnp.int32),
            VMEM((3, 3, CH), BF16),
            VMEM((3, 3, CH, CH), BF16),
            VMEM((4, 512, 512), BF16),
            VMEM((4, 256, WINDOW), BF16),
            VMEM((CH * MEL_SUB, model), BF16),
            VMEM((model,), F32),
            VMEM((model, 3 * local), BF16),
            VMEM((mp_count, local, half), BF16),
            VMEM((mp_count, local, half), BF16),
            VMEM((mp_count, per_block), jnp.int32),
            VMEM((256, MEL_HALF * CH), BF16),
            VMEM((30 * CH, 4 * CH), BF16),
            VMEM((CH * MEL_SUB, model), BF16),
            VMEM((utterances * SLOT_ROWS, 896), BF16),
            VMEM((slots, WINDOW), F32),
            VMEM((dp_count, capacity, WINDOW), BF16),
            VMEM((dp_count, capacity, WINDOW), BF16),
            VMEM((mp_count, per_block, WINDOW), BF16),
            VMEM((3, rows, 256), BF16),
            VMEM((rows, 384 + 3 * MEL_HALF * CH), BF16),
            VMEM((rows, CH * MEL_SUB), BF16),
            VMEM((rows, model), BF16),
            VMEM((rows, model), BF16),
            VMEM((rows, 3 * local), BF16),
            VMEM((mp_count, per_block, local), BF16),
            VMEM((mp_count, per_block, local), BF16),
            dma((15,)),
            dma,
            dma,
            dma((mp_count,)),
            dma((mp_count,)),
            dma((2, mp_count)),
            dma((2, mp_count)),
            dma((2, 2)),
            dma((2, 2)),
            dma((7,)),
            dma((7,)),
            dma((mp_count,)),
            dma((mp_count,)),
        ],
        compiler_params=pltpu.CompilerParams(
            vmem_limit_bytes=60 * 2**20, collective_id=0, has_side_effects=True
        ),
        name="encode",
    )(*operands)
    return encoded.reshape(1, 1, per_block, model)


def solution(mesh):
    return jax.shard_map(
        functools.partial(on_device, mesh.shape["dp"], mesh.shape["mp"]),
        mesh=mesh,
        in_specs=(
            P("dp", "mp", None, None),
            P("dp", "mp", None),
            P(),
            P(),
            P(),
            P(),
            P(None, None, "mp"),
            P("mp", None),
            P("dp", None, "mp", None),
            P("dp", "mp", None),
            P("dp", None, None),
        ),
        out_specs=P("dp", "mp", None, None),
        check_vma=False,
    )
```

```python
import functools
import math

import jax
import jax.numpy as jnp
import ml_dtypes
import numpy as np
from jax import lax
from jax.experimental import pallas as pl
from jax.experimental.pallas import tpu as pltpu
from jax.sharding import PartitionSpec as P

N_MEL = 80
N_FFT = 400
HOP = 160
HEAD_DIM = 64
SLOT_ROWS = 64
CH = 64
MEL_HALF = 40
MEL_SUB = 20
STEP = 4 * HOP
ROW = 4 * N_MEL
WINDOW = 2 * ROW
X_CHIPS = 4
MESH = pl.DeviceIdType.MESH
VMEM = pltpu.VMEM
BF16 = jnp.bfloat16
F32 = jnp.float32


def dft_table():
    position = np.arange(N_FFT)[:, None]
    harmonic = np.arange(256)[None, :]
    angles = 2.0 * math.pi * ((position * harmonic) % N_FFT) / N_FFT
    window = (0.5 - 0.5 * np.cos(2.0 * math.pi * position / N_FFT)) / math.sqrt(N_FFT)
    inside = harmonic <= N_FFT // 2
    base = np.concatenate(
        [np.where(inside, np.cos(angles), 0.0), np.where(inside, -np.sin(angles), 0.0)], axis=1
    )
    table = np.zeros((4, 512, 512))
    for r in range(4):
        table[r, 32 * r : 32 * r + N_FFT] = base * window
    return table.astype(ml_dtypes.bfloat16)


def mel_table():
    frequency = np.arange(N_FFT // 2 + 1) * (16000.0 / N_FFT)
    mel_top = 2595.0 * math.log10(1.0 + 8000.0 / 700.0)
    points = np.arange(N_MEL + 2) * (mel_top / (N_MEL + 1))
    hertz = 700.0 * (10.0 ** (points / 2595.0) - 1.0)
    lower, centre, upper = hertz[:-2], hertz[1:-1], hertz[2:]
    rising = (frequency[:, None] - lower) / (centre - lower)
    falling = (upper - frequency[:, None]) / (upper - centre)
    weights = np.maximum(0.0, np.minimum(rising, falling))
    table = np.zeros((4, 256, WINDOW))
    for r in range(4):
        for half in range(2):
            start = half * ROW + r * N_MEL
            table[r, : N_FFT // 2 + 1, start : start + N_MEL] = weights
    return table.astype(ml_dtypes.bfloat16)


def dot(a, b):
    return jnp.dot(a, b, preferred_element_type=F32)


def one_hot(condition):
    return condition.astype(F32).astype(BF16)


def iota(shape, dimension):
    return lax.broadcasted_iota(jnp.int32, shape, dimension)


def contract(a, b, dim_a, dim_b):
    return lax.dot_general(a, b, (((dim_a,), (dim_b,)), ((), ())), preferred_element_type=F32)


def solution_kernel(
    dp_count,
    mp_count,
    wave_hbm,
    lengths_hbm,
    picks_hbm,
    arrivals_hbm,
    first_hbm,
    second_hbm,
    dft_hbm,
    mel_hbm,
    weight_hbm,
    gain_hbm,
    attention_hbm,
    output_hbm,
    ids_hbm,
    encoded,
    wave,
    lengths,
    picks,
    arrivals,
    conv_first,
    conv_second,
    dft,
    mel,
    raw,
    norm_gain,
    attention,
    near,
    far,
    ids,
    first_table,
    second_table,
    weight,
    samples,
    slots_rows,
    outgoing,
    incoming,
    windows,
    shifted,
    hidden,
    features,
    embedded,
    normed,
    projected,
    sending,
    contexts,
    load_sems,
    exchange_send,
    exchange_recv,
    gather_send,
    gather_recv,
    near_send,
    near_recv,
    ring_send,
    ring_recv,
    far_send,
    far_recv,
    context_send,
    context_recv,
    pair_send,
    pair_recv,
):
    dp, me = lax.axis_index("dp"), lax.axis_index("mp")
    core = lax.rem(dp, 2)
    capacity = picks.shape[0]
    utterances = wave.shape[0]
    frames = utterances * SLOT_ROWS
    slots = dp_count * capacity
    per_block = windows.shape[1]
    rows = mp_count * per_block
    model = weight.shape[1]
    local = attention.shape[1] // 3
    half = model // 2
    width = MEL_HALF * CH

    own_output = output_hbm.at[:, pl.ds(pl.multiple_of(core * half, 128), half)]
    plan = [
        (wave_hbm, wave),
        (dft_hbm, dft),
        (mel_hbm, mel),
        (lengths_hbm, lengths),
        (picks_hbm, picks),
        (first_hbm, conv_first),
        (second_hbm, conv_second),
        (arrivals_hbm, arrivals),
        (ids_hbm, ids),
        (gain_hbm, norm_gain),
        (weight_hbm, raw),
        (own_output, near.at[0]),
    ]
    for part in range(3):
        plan.append((attention_hbm.at[part], attention.at[:, part * local : (part + 1) * local]))
    loads = [
        pltpu.make_async_copy(source, target, load_sems.at[index])
        for index, (source, target) in enumerate(plan)
    ]
    for load in loads[:5]:
        load.start()

    barrier = pltpu.get_barrier_semaphore()

    @pl.loop(1, dp_count)
    def _(d):
        pl.semaphore_signal(
            barrier, inc=1, device_id=(lax.rem(dp + d, dp_count), me), device_id_type=MESH
        )

    for d in range(1, mp_count):
        pl.semaphore_signal(
            barrier, inc=1, device_id=(dp, lax.rem(me + d, mp_count)), device_id_type=MESH
        )

    for load in loads[5:]:
        load.start()

    loads[0].wait()
    for s in range(SLOT_ROWS):
        samples[utterances * s : utterances * (s + 1), :] = wave[:, STEP * s : STEP * s + 896]
    loads[1].wait()
    loads[2].wait()
    energy = jnp.zeros((frames, WINDOW), F32)
    for r in range(4):
        spectrum = dot(samples[:, 128 * r : 128 * r + 512], dft[r])
        power = spectrum[:, :256] * spectrum[:, :256] + spectrum[:, 256:] * spectrum[:, 256:]
        energy += dot(power.astype(BF16), mel[r])
    loads[3].wait()
    row = iota((frames, 1), 0)
    limit = jnp.broadcast_to(lengths[0:1, 0:1], (frames, 1))
    for u in range(1, utterances):
        limit = jnp.where(row % utterances == u, lengths[0:1, u : u + 1], limit)
    image = jnp.where(row // utterances < limit, jnp.log(energy + 0.01), 0.0).astype(BF16)

    loads[4].wait()
    target = (dp + iota((slots, dp_count), 0) // capacity) % dp_count
    chosen = contract(
        one_hot(iota((slots, dp_count), 1) == target), picks[...].astype(F32).astype(BF16), 1, 1
    )
    chosen = jnp.where(
        iota((slots, capacity), 1) == iota((slots, capacity), 0) % capacity, chosen, 0.0
    )
    pick = jnp.sum(chosen, axis=1, keepdims=True).astype(jnp.int32)
    place = jnp.where(pick < 0, -SLOT_ROWS, pick % SLOT_ROWS * utterances + pick // SLOT_ROWS)
    column = iota((slots, frames), 1)
    own = dot(one_hot(column == place), image)
    earlier = dot(one_hot(column == place - utterances), image)
    slots_rows[...] = jnp.where(iota(own.shape, 1) < ROW, earlier, own).astype(BF16)
    for d in range(dp_count):
        slab = slots_rows[capacity * d : capacity * (d + 1), :]
        if d == 0:
            incoming[0] = slab
        else:
            outgoing[d] = slab

    pl.semaphore_wait(barrier, dp_count - 1 + mp_count - 1)

    def exchange(slab, d):
        return pltpu.make_async_remote_copy(
            src_ref=outgoing.at[slab],
            dst_ref=incoming.at[slab],
            send_sem=exchange_send,
            recv_sem=exchange_recv,
            device_id=(lax.rem(dp + d, dp_count), me),
            device_id_type=MESH,
        )

    def to_lane(source, target, send_sem, recv_sem, d):
        return pltpu.make_async_remote_copy(
            src_ref=source,
            dst_ref=target,
            send_sem=send_sem,
            recv_sem=recv_sem,
            device_id=(dp, lax.rem(me + d, mp_count)),
            device_id_type=MESH,
        )

    stride = dp_count // X_CHIPS
    ring = dp // stride
    quarter = local // 4
    parity = lax.rem(ring, 2)

    def quarter_rows(side, c, start=0, size=quarter):
        first = (2 * side + c) * quarter + start
        return pl.ds(pl.multiple_of(first, 16), size)

    def part_copy(c, d):
        rows = quarter_rows(parity, c)
        return to_lane(
            output_hbm.at[rows, pl.ds(pl.multiple_of(core * half, 128), half)],
            near.at[mp_count - d, rows],
            near_send.at[c, d],
            near_recv.at[c, d],
            d,
        )

    def ring_copy(c, step, side):
        rows = quarter_rows(side, c, step * (quarter // 2), quarter // 2)
        return pltpu.make_async_remote_copy(
            src_ref=near.at[1:, rows],
            dst_ref=near.at[1:, rows],
            send_sem=ring_send.at[c, step],
            recv_sem=ring_recv.at[c, step],
            device_id=(lax.rem(dp + (1 - 2 * step) * stride + dp_count, dp_count), me),
            device_id_type=MESH,
        )

    def to_sibling(index):
        if index == 0:
            source, target = near.at[0], far.at[0]
        elif index < 3:
            rows = quarter_rows(parity, index - 1)
            source, target = near.at[1:, rows], far.at[1:, rows]
        else:
            c, step = (index - 3) // 2, (index - 3) % 2
            rows = quarter_rows(1 - parity, c, step * (quarter // 2), quarter // 2)
            source, target = near.at[1:, rows], far.at[1:, rows]
        return pltpu.make_async_remote_copy(
            src_ref=source,
            dst_ref=target,
            send_sem=far_send.at[index],
            recv_sem=far_recv.at[index],
            device_id=(dp + 1 - 2 * core, me),
            device_id_type=MESH,
        )

    def pass_on(c):
        for d in range(1, mp_count):
            part_copy(c, d).wait_recv()
        for step in range(2):
            ring_copy(c, step, parity).start()
        to_sibling(1 + c).start()

    def share_ring(c):
        for step in range(2):
            ring_copy(c, step, 1 - parity).wait_recv()
            to_sibling(3 + 2 * c + step).start()

    @pl.loop(1, dp_count)
    def _(d):
        exchange(d, d).start()

    for d in range(1, mp_count):
        part_copy(0, d).start()

    loads[5].wait()
    loads[6].wait()
    twice = one_hot(iota((CH, 2 * CH), 0) == iota((CH, 2 * CH), 1) % CH)
    taps = [dot(conv_first[d], twice) for d in range(3)]
    first_table[3 * N_MEL :, :] = jnp.zeros((256 - 3 * N_MEL, width), BF16)
    offset = iota((N_MEL, 2 * CH), 0) - 2 * (iota((N_MEL, 2 * CH), 1) // CH) + 1
    for n in range(MEL_HALF // 2):
        for t in range(3):
            block = jnp.zeros(offset.shape, F32)
            for d in range(3):
                block = jnp.where(offset - 4 * n == d, taps[d][t : t + 1, :], block)
            first_table[t * N_MEL : (t + 1) * N_MEL, 2 * CH * n : 2 * CH * (n + 1)] = block.astype(BF16)
    spread = one_hot(iota((CH, 4 * CH), 0) == iota((CH, 4 * CH), 1) // 4)
    sub_band = iota((CH, 4 * CH), 1) % 4
    for t in range(3):
        wide = [contract(conv_second[d, t], spread, 0, 0) for d in range(3)]
        for k in range(10):
            block = jnp.zeros((CH, 4 * CH), F32)
            for d in range(3):
                block = jnp.where(2 * sub_band + d + 1 == k, wide[d], block)
            start = k // 2 * 384 + t * 128 + k % 2 * CH
            second_table[start : start + CH, :] = block.astype(BF16)
    span = 16 * MEL_SUB
    out_row, in_row = iota((span, span), 0), iota((span, span), 1)
    source = (out_row % 64 // 4) * MEL_SUB + out_row // 64 * 4 + out_row % 4
    order = one_hot(in_row == source)
    loads[10].wait()
    for block in range(4):
        value = dot(order, raw[block * span : (block + 1) * span, :]).astype(BF16)
        for g in range(5):
            weight[256 * g + 64 * block : 256 * g + 64 * (block + 1), :] = value[64 * g : 64 * (g + 1), :]
    for d in range(1, mp_count):
        part_copy(1, d).start()
    shifted[:, :, 3 * N_MEL :] = jnp.zeros((3, rows, 256 - 3 * N_MEL), BF16)
    hidden[:, :384] = jnp.zeros((rows, 384), BF16)

    loads[7].wait()
    loads[8].wait()
    loads[9].wait()
    loads[11].wait()
    loads[12].wait()
    loads[13].wait()
    loads[14].wait()
    arrival = arrivals[...]
    position = (dp + dp_count - arrival // capacity) % dp_count * capacity + arrival % capacity
    take = (iota((slots, per_block), 0) == position).astype(F32)
    take = jnp.transpose(take).astype(BF16)
    to_sibling(0).start()
    pass_on(0)

    all_slabs = exchange(pl.ds(1, dp_count - 1), 1)
    all_slabs.wait_recv()
    for d in range(dp_count):
        slots_rows[capacity * d : capacity * (d + 1), :] = incoming[d]
    windows[0] = dot(take, slots_rows[...]).astype(BF16)

    last = mp_count - 1
    window_out = {
        d: to_lane(
            windows.at[0], windows.at[mp_count - d], gather_send.at[d], gather_recv.at[mp_count - d], d
        )
        for d in (1, last, 2)
    }
    window_out[1].start()
    window_out[last].start()

    def wait_window(d):
        to_lane(windows.at[0], windows.at[d], gather_send.at[d], gather_recv.at[d], d).wait_recv()

    def convolve(start, stop, image):
        span = slice(start, stop)
        for t in range(3):
            first = (1 + 2 * t) * N_MEL
            shifted[t, span, : 3 * N_MEL] = image[:, first : first + 3 * N_MEL]
        for t in range(3):
            for n in range(width // 256):
                value = dot(shifted[t, span, :], first_table[:, n * 256 : (n + 1) * 256])
                value = jnp.maximum(value, 0.0).astype(BF16)
                for pair in range(2):
                    lanes = 384 * (1 + 2 * n + pair) + 128 * t
                    hidden[span, lanes : lanes + 128] = value[:, 128 * pair : 128 * (pair + 1)]
        for g in range(5):
            value = dot(hidden[span, 1536 * g : 1536 * g + 1920], second_table[...])
            features[span, 256 * g : 256 * (g + 1)] = jnp.maximum(value, 0.0).astype(BF16)

    def project(start, stop):
        span = slice(start, stop)
        for n in range(model // 256):
            embedded[span, n * 256 : (n + 1) * 256] = dot(
                features[span, :], weight[:, n * 256 : (n + 1) * 256]
            ).astype(BF16)
        gain = norm_gain[...].reshape(1, model)
        for b in range(start, stop, per_block):
            values = embedded[b : b + per_block, :].astype(F32)
            centre = values - jnp.mean(values, axis=-1, keepdims=True)
            variance = jnp.mean(centre * centre, axis=-1, keepdims=True)
            normed[b : b + per_block, :] = (centre * lax.rsqrt(variance + 1e-05) * gain).astype(BF16)
        for start in range(0, 3 * local, 256):
            lanes = slice(start, min(start + 256, 3 * local))
            projected[span, lanes] = dot(normed[span, :], attention[:, lanes]).astype(BF16)

    lower = iota((per_block, 128), 1) < HEAD_DIM
    zero = jnp.zeros((per_block, 128), BF16)

    def attend(b, target, after=None):
        d = (0, 1, last, 2)[b]
        block_ids = ids[pl.ds(lax.rem(me + d, mp_count), 1), :]
        across = jnp.broadcast_to(block_ids, (per_block, per_block))
        same = across == jnp.transpose(across)
        span = slice(b * per_block, (b + 1) * per_block)
        for pair in range(local // 128):
            lanes = slice(pair * 128, (pair + 1) * 128)
            query = projected[span, lanes]
            key = projected[span, local + pair * 128 : local + (pair + 1) * 128]
            value = projected[span, 2 * local + pair * 128 : 2 * local + (pair + 1) * 128]
            key_pair = jnp.concatenate(
                [jnp.where(lower, key, zero), jnp.where(lower, zero, key)], axis=0
            )
            value_pair = jnp.concatenate(
                [jnp.where(lower, value, zero), jnp.where(lower, zero, value)], axis=0
            )
            scores = contract(query, key_pair, 1, 1) * (1.0 / math.sqrt(HEAD_DIM))
            weights = []
            for side in range(2):
                part = jnp.where(same, scores[:, side * per_block : (side + 1) * per_block], -jnp.inf)
                largest = jnp.max(part, axis=-1, keepdims=True)
                exponent = jnp.exp(part - largest)
                total = jnp.sum(exponent, axis=-1, keepdims=True)
                weights.append((exponent / total).astype(BF16))
            target[b, :, lanes] = dot(jnp.concatenate(weights, axis=1), value_pair).astype(BF16)
            if after is not None:
                after(pair, lanes)

    context_out = {}

    def share_contexts(d, block):
        attend(block, sending)
        context_out[d] = to_lane(
            sending.at[block],
            contexts.at[mp_count - d],
            context_send.at[d],
            context_recv.at[mp_count - d],
            d,
        )
        context_out[d].start()

    convolve(0, per_block, windows[0])
    pass_on(1)
    project(0, per_block)
    attend(0, contexts)
    all_slabs.wait_send()
    for c in range(2):
        for d in range(1, mp_count):
            part_copy(c, d).wait_send()
    wait_window(1)
    wait_window(last)
    window_out[2].start()
    image = jnp.concatenate([windows[1], windows[last]], axis=0)
    convolve(per_block, 3 * per_block, image)
    project(per_block, 3 * per_block)
    share_contexts(1, 1)
    share_contexts(last, 2)
    wait_window(2)
    convolve(3 * per_block, rows, windows[2])
    share_ring(0)
    project(3 * per_block, rows)
    share_ring(1)

    def pair_copy(pair, lanes):
        return to_lane(
            sending.at[3, :, lanes],
            contexts.at[mp_count - 2, :, lanes],
            pair_send.at[pair],
            pair_recv.at[pair],
            2,
        )

    attend(3, sending, lambda pair, lanes: pair_copy(pair, lanes).start())
    pairs = [pair_copy(pair, slice(pair * 128, (pair + 1) * 128)) for pair in range(local // 128)]
    for copy in list(window_out.values()) + [context_out[1], context_out[last]]:
        copy.wait_send()
    for c in range(2):
        for step in range(2):
            ring_copy(c, step, parity).wait_send()
    for index in range(7):
        to_sibling(index).wait_send()
    for index in range(7):
        to_sibling(index).wait_recv()

    sides = [embedded[:per_block, pl.ds(pl.multiple_of(index * half, 128), half)].astype(F32) for index in (core, 1 - core)]
    for d in (0, 1, last, 2):
        if d == 2:
            for copy in pairs:
                copy.wait_recv()
        elif d:
            to_lane(sending.at[d], contexts.at[d], context_send.at[d], context_recv.at[d], d).wait_recv()
        for index, part in enumerate((near, far)):
            sides[index] += dot(contexts[d], part[d])
    for index, value in zip((core, 1 - core), sides):
        encoded[:, pl.ds(pl.multiple_of(index * half, 128), half)] = value.astype(BF16)

    for copy in pairs:
        copy.wait_send()


def on_device(
    dp_count,
    mp_count,
    waveform,
    lengths,
    conv_first,
    conv_second,
    input_weight,
    norm_gain,
    attention_in,
    attention_out,
    send_slots,
    receive_slots,
    segment_ids,
):
    capacity = send_slots.shape[3]
    utterances = waveform.shape[2]
    per_block = receive_slots.shape[2]
    model = input_weight.shape[1]
    local = attention_in.shape[2]
    half = model // 2
    rows = mp_count * per_block
    slots = dp_count * capacity
    dma = pltpu.SemaphoreType.DMA
    operands = (
        waveform[0, 0],
        lengths[0],
        send_slots[0, :, 0, :].transpose(1, 0),
        receive_slots[0],
        conv_first.transpose(1, 2, 3, 0)[0],
        conv_second.transpose(2, 3, 0, 1),
        jnp.asarray(dft_table()),
        jnp.asarray(mel_table()),
        input_weight,
        norm_gain,
        attention_in.transpose(1, 0, 2),
        attention_out,
        segment_ids[0],
    )
    encoded = pl.pallas_call(
        functools.partial(solution_kernel, dp_count, mp_count),
        out_shape=jax.ShapeDtypeStruct((per_block, model), BF16),
        in_specs=[pl.BlockSpec(memory_space=pltpu.HBM)] * len(operands),
        out_specs=pl.BlockSpec(memory_space=VMEM),
        scratch_shapes=[
            VMEM(waveform.shape[2:], BF16),
            VMEM((1, utterances), jnp.int32),
            VMEM((capacity, dp_count), jnp.int32),
            VMEM((1, per_block), jnp.int32),
            VMEM((3, 3, CH), BF16),
            VMEM((3, 3, CH, CH), BF16),
            VMEM((4, 512, 512), BF16),
            VMEM((4, 256, WINDOW), BF16),
            VMEM((CH * MEL_SUB, model), BF16),
            VMEM((model,), F32),
            VMEM((model, 3 * local), BF16),
            VMEM((mp_count, local, half), BF16),
            VMEM((mp_count, local, half), BF16),
            VMEM((mp_count, per_block), jnp.int32),
            VMEM((256, MEL_HALF * CH), BF16),
            VMEM((30 * CH, 4 * CH), BF16),
            VMEM((CH * MEL_SUB, model), BF16),
            VMEM((utterances * SLOT_ROWS, 896), BF16),
            VMEM((slots, WINDOW), BF16),
            VMEM((dp_count, capacity, WINDOW), BF16),
            VMEM((dp_count, capacity, WINDOW), BF16),
            VMEM((mp_count, per_block, WINDOW), BF16),
            VMEM((3, rows, 256), BF16),
            VMEM((rows, 384 + 3 * MEL_HALF * CH), BF16),
            VMEM((rows, CH * MEL_SUB), BF16),
            VMEM((rows, model), BF16),
            VMEM((rows, model), BF16),
            VMEM((rows, 3 * local), BF16),
            VMEM((mp_count, per_block, local), BF16),
            VMEM((mp_count, per_block, local), BF16),
            dma((15,)),
            dma,
            dma,
            dma((mp_count,)),
            dma((mp_count,)),
            dma((2, mp_count)),
            dma((2, mp_count)),
            dma((2, 2)),
            dma((2, 2)),
            dma((7,)),
            dma((7,)),
            dma((mp_count,)),
            dma((mp_count,)),
            dma((local // 128,)),
            dma((local // 128,)),
        ],
        compiler_params=pltpu.CompilerParams(
            vmem_limit_bytes=60 * 2**20, collective_id=0, has_side_effects=True
        ),
        name="encode",
    )(*operands)
    return encoded.reshape(1, 1, per_block, model)


def solution(mesh):
    return jax.shard_map(
        functools.partial(on_device, mesh.shape["dp"], mesh.shape["mp"]),
        mesh=mesh,
        in_specs=(
            P("dp", "mp", None, None),
            P("dp", "mp", None),
            P(),
            P(),
            P(),
            P(),
            P(None, None, "mp"),
            P("mp", None),
            P("dp", None, "mp", None),
            P("dp", "mp", None),
            P("dp", None, None),
        ),
        out_specs=P("dp", "mp", None, None),
        check_vma=False,
    )
```
